32 devices in a mesh: grp: 2 (over x), brick: 8 (over z, y), cuts: 2 (over core).
Axes of the slice: x: 2, y: 2, z: 4, core: 2. Of those that a mesh axis runs over, the one named last changes fastest.
Arguments:
- initial: float32 [3, 512, 5120], P(None, ('grp', 'brick')), parts along dimension 1, may hold values from -3 to 3
- depth: float32 [256, 5120], P('brick'), may hold values from 0.5 to 2.5
- mask: int32 [256, 5120], P('brick'), may hold values 0 or 1
Outputs:
- ends: float32 [2, 3, 512, 5120], P('cuts', None, ('grp', 'brick')), parts along dimension 2
The draws below stay inside these ranges and needn't reach their ends.
There are 2 independent parts, one for each index of `grp`. The reference program is written for one: setup_inputs(seed, part) draws one part's arguments, and reference() takes and returns one part's arrays. A program takes and returns all parts, laid end to end along the dimension named above; an argument that names none is the same for every part. Nothing has to cross between parts.
Inputs may be any that keep to these rules, and one draw needn't show every extreme that they name: `mask`: 1 marks an ocean cell, 0 land.
All inputs are finite; a program needn't handle non-finite values. No bound on the sum of `mask` on one device may be relied on, other than what follows from the above.
Results may differ from the reference program's by a relative error of at most 0.0001.
Values sent between devices are 32-bit elements; how exact they have to be, the bound alone decides.
No kernel may reach another device: no remote copies, remote signals or barrier semaphores. Data moves between devices by JAX's collectives and lax.ppermute only.
A program may use at most 64 MiB of HBM per device.

```python
import math
import jax
import jax.numpy as jnp
from jax import lax

NY = 5120
ITERS = 1
SLICES = 2
NX = 256


def with_ends(array, stream_key, smallest, high):
    index_at = [jax.random.randint(jax.random.fold_in(stream_key, axis), (), 0, length) for axis, length in enumerate(array.shape)]
    widest = array.shape.index(max(array.shape))
    beside = index_at[:widest] + [(index_at[widest] + 1) % array.shape[widest]] + index_at[widest + 1:]
    return array.at[tuple(index_at)].set(smallest).at[tuple(beside)].set(high)


def level_of(own_key, dims, pieces, smallest, largest):
    def one(axis_at, blocks):
        draws = jax.random.uniform(jax.random.fold_in(jax.random.fold_in(own_key, 6), axis_at), (blocks,), jnp.float32, smallest / len(pieces), largest / len(pieces))
        return jnp.repeat(jnp.exp(draws), dims[axis_at] // blocks).reshape((-1,) + (1,) * (len(dims) - axis_at - 1))

    level = one(*pieces[0])
    for cut in pieces[1:]:
        level = level * one(*cut)
    return level


def gaussian(rng, dims, deviation, limit, shards=(), held_as=jnp.bfloat16):
    loudness = level_of(rng, dims, shards, -0.22, 0.18) if shards else 1.0
    drawn = jax.random.normal(rng, dims, jnp.float32) * deviation * loudness
    return jnp.minimum(jnp.maximum(drawn, -limit), limit).astype(held_as)


def setup_inputs(seed: int = 0, part: int = 0) -> dict:
    splits = jax.random.split(jax.random.key(seed), 4)
    part_splits = jax.random.split(jax.random.fold_in(splits[3], part), 4)
    return {
        "initial": gaussian(part_splits[0], (3, NX, NY), 0.5, 3.0, ((1, 8),), jnp.float32),
        "depth": jnp.clip(jnp.exp(math.log(2.5) - 1.609438 * jax.random.uniform(splits[1], (NX, NY), jnp.float32) ** level_of(splits[1], (NX, NY), ((0, 8),), -0.2, 0.2)), 0.5, 2.5),
        "mask": with_ends((jax.random.randint(splits[2], (NX, NY), 0, 5) < 4).astype(jnp.int32), jax.random.fold_in(splits[2], 1), 0, 1),
    }


COURANT = 0.2
DIFFUSION = 0.05
GRAVITY = 1.0
FRICTION = 0.01
CORIOLIS = 0.5
FINE_TIME = 0.2
COARSE_TIME = 0.4


def restrict(fields):
    extent = fields.shape
    blocks = fields.reshape(extent[:-2] + (extent[-2] // 2, 2, extent[-1] // 2, 2))
    return jnp.sum(blocks, axis=(-3, -1)) * 0.25


def prolong(fields):
    return jnp.repeat(jnp.repeat(fields, 2, axis=-2), 2, axis=-1)


def row_diff(padded):
    return (padded[..., 2:, :] - padded[..., :-2, :]) * 0.5


def col_diff(center):
    return (jnp.roll(center, -1, axis=-1) - jnp.roll(center, 1, axis=-1)) * 0.5


def diffuse(padded):
    center = padded[..., 1:-1, :]
    return padded[..., 2:, :] + padded[..., :-2, :] + jnp.roll(center, 1, axis=-1) + jnp.roll(center, -1, axis=-1) - 4.0 * center


def advance(padded, depth_pad, wet_pad, coriolis, keep, time_step):
    height_pad = padded[:, 0]
    east_pad = padded[:, 1]
    north_pad = padded[:, 2]
    height = height_pad[:, 1:-1]
    east_flow = east_pad[:, 1:-1]
    north_flow = north_pad[:, 1:-1]
    column_depth = depth_pad + height_pad
    east_flux = column_depth * east_pad
    north_flux = (column_depth * north_pad)[:, 1:-1]
    new_height = height - COURANT * (row_diff(east_flux) + col_diff(north_flux)) + DIFFUSION * diffuse(height_pad)
    new_east = (east_flow - COURANT * (east_flow * row_diff(east_pad) + north_flow * col_diff(east_flow))
                + time_step * coriolis * north_flow - COURANT * GRAVITY * row_diff(height_pad)
                - time_step * FRICTION * east_flow + DIFFUSION * diffuse(east_pad))
    new_north = (north_flow - COURANT * (east_flow * row_diff(north_pad) + north_flow * col_diff(north_flow))
                 - time_step * coriolis * east_flow - COURANT * GRAVITY * col_diff(height)
                 - time_step * FRICTION * north_flow + DIFFUSION * diffuse(north_pad))
    wet_mask = wet_pad[1:-1]
    result = jnp.stack([new_height, new_east * wet_mask, new_north * wet_mask], axis=1)
    if keep is not None:
        result = result * keep
    return result


def pad_rows(states):
    return jnp.pad(states, ((0, 0), (0, 0), (1, 1), (0, 0)))


def reference(initial, depth, mask):
    wet_mask = mask.astype(jnp.float32)
    depth_pad = jnp.pad(depth, ((1, 1), (0, 0)))
    wet_pad = jnp.pad(wet_mask, ((1, 1), (0, 0)))
    coarse_depth = jnp.pad(restrict(depth), ((1, 1), (0, 0)))
    coarse_wet = jnp.pad(restrict(wet_mask), ((1, 1), (0, 0)))
    fine_rows = jnp.arange(NX).astype(jnp.float32)
    fine_cor = (CORIOLIS * ((2.0 * fine_rows + 1.0) / NX - 1.0))[:, None]
    coarse_rows = jnp.arange(NX // 2).astype(jnp.float32)
    coarse_cor = (CORIOLIS * ((4.0 * coarse_rows + 2.0) / NX - 1.0))[:, None]

    def fine_flow(single):
        states = single[None]
        for repeat_index in range(2):
            states = advance(pad_rows(states), depth_pad, wet_pad, fine_cor, None, FINE_TIME)
        return states[0]

    def coarse_flow(single):
        return advance(pad_rows(single[None]), coarse_depth, coarse_wet, coarse_cor, None, COARSE_TIME)[0]

    start = restrict(initial)

    def sweep(deltas):
        def onward(current, correction):
            current = coarse_flow(current) + correction
            return current, current
        _, results = lax.scan(onward, start, deltas)
        return results

    zeros = jnp.zeros((SLICES,) + start.shape, jnp.float32)
    ends = prolong(sweep(zeros))
    for iteration in range(ITERS):
        starts = jnp.concatenate([initial[None], ends[:-1]], axis=0)
        fine_ends = lax.map(fine_flow, starts)
        coarse_ends = lax.map(lambda single: coarse_flow(restrict(single)), starts)
        rfine = restrict(fine_ends)
        updated = sweep(rfine - coarse_ends)
        ends = fine_ends + prolong(updated - rfine)
    return ends
```

```python
import functools

import jax
import jax.numpy as jnp
from jax import lax
from jax.experimental import pallas as pl
from jax.experimental.pallas import tpu as pltpu
from jax.sharding import PartitionSpec as P


COURANT = 0.2
DIFFUSION = 0.05
FRICTION = 0.01
CORIOLIS = 0.5
FINE_TIME = 0.2
COARSE_TIME = 0.4
SUB, LANES = 8, 128
HALO = 4
PER = 5
PACKED = HALO * PER - 1
VMEM_LIMIT = 40 * 1024 * 1024


def next_col(x, amount, edge):
    turned = [pltpu.roll(a, LANES - amount, 1) for a in x]
    turned.append(pltpu.roll(turned[0], SUB - 1, 0))
    return [jnp.where(edge, turned[j + 1], turned[j]) for j in range(len(x))]


def prev_col(x, amount, edge):
    turned = [pltpu.roll(a, amount, 1) for a in x]
    turned.insert(0, pltpu.roll(turned[-1], 1, 0))
    return [jnp.where(edge, turned[j], turned[j + 1]) for j in range(len(x))]


def lane_ids():
    return lax.broadcasted_iota(jnp.int32, (SUB, LANES), 1)


def step(state, depth, wet, turn, dt, cols):
    (eb, ub, vb), (e, u, v), (ea, ua, va) = state
    hb, h, ha = depth
    lane = lane_ids()
    last, first = lane >= LANES - cols, lane < cols
    nj = len(e)
    g = [(h[j] + e[j]) * v[j] for j in range(nj)]
    e_r, e_l = next_col(e, cols, last), prev_col(e, cols, first)
    u_r, u_l = next_col(u, cols, last), prev_col(u, cols, first)
    v_r, v_l = next_col(v, cols, last), prev_col(v, cols, first)
    g_r, g_l = next_col(g, cols, last), prev_col(g, cols, first)
    half = 0.5 * COURANT
    keep_e = 1.0 - 4.0 * DIFFUSION
    keep = 1.0 - dt * FRICTION - 4.0 * DIFFUSION
    new_e, new_u, new_v = [], [], []
    for j in range(nj):
        flux = ((ha[j] + ea[j]) * ua[j] - (hb[j] + eb[j]) * ub[j]) + (g_r[j] - g_l[j])
        around = (ea[j] + eb[j]) + (e_r[j] + e_l[j])
        new_e.append(keep_e * e[j] + (DIFFUSION * around - half * flux))
        a, b = half * u[j], half * v[j]
        a_up, a_dn, b_up, b_dn = DIFFUSION - a, DIFFUSION + a, DIFFUSION - b, DIFFUSION + b
        nu = (keep * u[j] + turn * v[j]) - half * (ea[j] - eb[j])
        nu = nu + ((ua[j] * a_up + ub[j] * a_dn) + (u_r[j] * b_up + u_l[j] * b_dn))
        nv = (keep * v[j] - turn * u[j]) - half * (e_r[j] - e_l[j])
        nv = nv + ((va[j] * a_up + vb[j] * a_dn) + (v_r[j] * b_up + v_l[j] * b_dn))
        new_u.append(nu * wet[j])
        new_v.append(nv * wet[j])
    return new_e, new_u, new_v


def average(low, high):
    even = lane_ids() % 2 == 0
    out = []
    for a, b in zip(low, high):
        s = a + b
        out.append((s + jnp.where(even, pltpu.roll(s, LANES - 1, 1), pltpu.roll(s, 1, 1))) * 0.25)
    return out


def rows_of(ref, *at):
    return [ref[(*at, j)] for j in range(ref.shape[-3])]


def put(ref, at, row):
    for j, a in enumerate(row):
        ref[(*at, j)] = a


def three(ref, at):
    return tuple(rows_of(ref, at, k) for k in range(3))


def put_three(ref, at, rows):
    for k, row in enumerate(rows):
        put(ref, (at, k), row)


def scaled(rows, factor):
    e, u, v = rows
    return [a * factor for a in e], u, v


def turning(row, first_row, scale, all_rows, dt):
    y = (first_row + row).astype(jnp.float32) * (2.0 * scale) + scale
    return (dt * CORIOLIS) * (y * (1.0 / all_rows) - 1.0)


def tile_row(nj, row, j):
    wide = nj * SUB
    return pl.ds((row // SUB) * (wide * SUB) + row % SUB + j * SUB, SUB, stride=nj * SUB)


def pack_kernel(nj, initial, depth, mask, out, initial_v, depth_v, mask_v, sems):
    lane = lax.axis_index("cuts")
    tile = nj * SUB * SUB
    high = initial.shape[1] // tile - 1
    start = pl.multiple_of(jnp.where(lane == 0, high, 0) * tile, tile)
    copies = [
        pltpu.make_async_copy(initial.at[:, pl.ds(start, tile), :], initial_v, sems.at[0]),
        pltpu.make_async_copy(depth.at[pl.ds(start, tile), :], depth_v, sems.at[1]),
        pltpu.make_async_copy(mask.at[pl.ds(start, tile), :], mask_v, sems.at[2]),
    ]
    for copy in copies:
        copy.start()
    for copy in copies:
        copy.wait()

    def fill(row_of):
        for d in range(HALO):
            for j in range(nj):
                at = tile_row(nj, row_of(d), j)
                for k in range(3):
                    out[d * PER + k, j] = initial_v[k, at, :]
                out[d * PER + 3, j] = depth_v[at, :]
                if d < HALO - 1:
                    out[d * PER + 4, j] = mask_v[at, :].astype(jnp.float32)

    pl.when(lane == 0)(lambda: fill(lambda d: SUB - 1 - d))
    pl.when(lane != 0)(lambda: fill(lambda d: d))


MID_INIT, MID_DEPTH, MID_WET, MID_ONE, MID_RF, MID_C1, MID_PONE = 0, 12, 18, 22, 28, 34, 40
MID = 46


def middle_kernel(nj, bricks, initial, depth, mask, out, mid, ini, hw, s1, s2, rc, rhw, c1, p1, dif):
    lane = lax.axis_index("cuts")
    brick = lax.axis_index("brick")
    n = ini.shape[0]
    m = n // 2
    all_rows = n * bricks

    def own(side, i, count=n):
        return i if side == 0 else count - 1 - i

    def load(t, carry):
        for r in range(SUB):
            row = t * SUB + r
            for j in range(nj):
                at = pl.ds(t * (nj * SUB * SUB) + r + j * SUB, SUB, stride=nj * SUB)
                for k in range(3):
                    ini[row, k, j] = initial[k, at, :]
                hw[row, 0, j] = depth[at, :]
                hw[row, 1, j] = mask[at, :].astype(jnp.float32)
        return carry

    lax.fori_loop(0, n // SUB, load, 0)

    def h3(row):
        return tuple(rows_of(hw, row + d, 0) for d in (-1, 0, 1))

    def fine(src, dst):
        def body(row, carry):
            state = tuple(three(src, row + d) for d in (-1, 0, 1))
            turn = turning(row, brick * n, 1.0, all_rows, FINE_TIME)
            put_three(dst, row, step(state, h3(row), rows_of(hw, row, 1), turn, FINE_TIME, 1))
            return carry

        return body

    lax.fori_loop(1, n - 1, fine(ini, s1), 0)
    lax.fori_loop(2, n - 2, fine(s1, s2), 0)

    for side in (0, 1):
        for i in range(4):
            put_three_mid(mid, side, MID_INIT + 3 * i, three(ini, own(side, i)))
            put(mid, (side, MID_WET + i), rows_of(hw, own(side, i), 1))
        for i in range(6):
            put(mid, (side, MID_DEPTH + i), rows_of(hw, own(side, i), 0))
        for i in (1, 2):
            put_three_mid(mid, side, MID_ONE + 3 * (i - 1), three(s1, own(side, i)))

    def emit(row, rows):
        for k in range(3):
            for j in range(nj):
                at = pl.ds((row // SUB) * (nj * SUB * SUB) + row % SUB + j * SUB, SUB, stride=nj * SUB)
                out[k, at, :] = rows[k][j]

    @pl.when(lane == 0)
    def _():
        def body(row, carry):
            emit(row, three(s2, row))
            return carry

        lax.fori_loop(2, n - 2, body, 0)

    @pl.when(lane != 0)
    def _():
        def restrict(row, carry):
            lo, hi = three(ini, 2 * row), three(ini, 2 * row + 1)
            put_three(rc, row, [average(a, b) for a, b in zip(lo, hi)])
            for k in range(2):
                put(rhw, (row, k), average(rows_of(hw, 2 * row, k), rows_of(hw, 2 * row + 1, k)))
            return carry

        lax.fori_loop(0, m, restrict, 0)

        def coarse(src, row):
            state = tuple(three(src, row + d) for d in (-1, 0, 1))
            heights = tuple(rows_of(rhw, row + d, 0) for d in (-1, 0, 1))
            turn = turning(row, brick * m, 2.0, all_rows, COARSE_TIME)
            return step(state, heights, rows_of(rhw, row, 1), turn, COARSE_TIME, 2)

        def first(row, carry):
            put_three(c1, row, coarse(rc, row))
            return carry

        lax.fori_loop(1, m - 1, first, 0)

        def again(row, carry):
            lo, hi = three(s2, 2 * row), three(s2, 2 * row + 1)
            put_three(rc, row, [average(a, b) for a, b in zip(lo, hi)])
            return carry

        lax.fori_loop(1, m - 1, again, 0)
        for side in (0, 1):
            for i in (1, 2):
                put_three_mid(mid, side, MID_RF + 3 * (i - 1), three(rc, own(side, i, m)))
                put_three_mid(mid, side, MID_C1 + 3 * (i - 1), three(c1, own(side, i, m)))

        def correct(row, carry):
            fresh, old = coarse(rc, row), coarse(c1, row)
            put_three(dif, row, [[a - b for a, b in zip(x, y)] for x, y in zip(fresh, old)])
            return carry

        lax.fori_loop(2, m - 2, correct, 0)

        def prolonged(row, carry):
            state = tuple(three(c1, (row + d) // 2) for d in (-1, 0, 1))
            turn = turning(row, brick * n, 1.0, all_rows, FINE_TIME)
            put_three(p1, row, step(state, h3(row), rows_of(hw, row, 1), turn, FINE_TIME, 1))
            return carry

        lax.fori_loop(3, n - 3, prolonged, 0)
        for side in (0, 1):
            for i in (3, 4):
                put_three_mid(mid, side, MID_PONE + 3 * (i - 3), three(p1, own(side, i)))

        def last(row, carry):
            state = tuple(three(p1, row + d) for d in (-1, 0, 1))
            turn = turning(row, brick * n, 1.0, all_rows, FINE_TIME)
            rows = step(state, h3(row), rows_of(hw, row, 1), turn, FINE_TIME, 1)
            add = three(dif, row // 2)
            emit(row, [[a + b for a, b in zip(x, y)] for x, y in zip(rows, add)])
            return carry

        lax.fori_loop(4, n - 4, last, 0)


def put_three_mid(mid, side, at, rows):
    for k, row in enumerate(rows):
        put(mid, (side, at + k), row)


def edge_kernel(nj, bricks, n, low1, high1, low0, high0, mid, before, out, halo, midv, tiles, sems):
    lane = lax.axis_index("cuts")
    brick = lax.axis_index("brick")
    all_rows = n * bricks
    m = n // 2
    tile = nj * SUB * SUB
    high_tile = (n // SUB - 1) * tile
    spots = (0, high_tile)
    fetch = [pltpu.make_async_copy(mid.at[s], midv.at[s], sems.at[s]) for s in (0, 1)]
    fetch += [
        pltpu.make_async_copy(before.at[:, pl.ds(spots[s], tile), :], tiles.at[s], sems.at[2 + s])
        for s in (0, 1)
    ]
    for copy in fetch:
        copy.start()

    def halos(low, high):
        got = [pltpu.make_async_copy(a, halo.at[s], sems.at[4 + s]) for s, a in enumerate((low, high))]
        for copy in got:
            copy.start()
        for copy in got:
            copy.wait()

    pl.when(lane == 0)(lambda: halos(low0, high0))
    pl.when(lane != 0)(lambda: halos(low1, high1))
    for copy in fetch:
        copy.wait()

    def initial(s, i):
        if i < 0:
            return tuple(rows_of(halo, s, (-1 - i) * PER + k) for k in range(3))
        return tuple(rows_of(midv, s, MID_INIT + 3 * i + k) for k in range(3))

    def depth(s, i):
        return rows_of(halo, s, (-1 - i) * PER + 3) if i < 0 else rows_of(midv, s, MID_DEPTH + i)

    def wet(s, i):
        return rows_of(halo, s, (-1 - i) * PER + 4) if i < 0 else rows_of(midv, s, MID_WET + i)

    def kept(s, base):
        return tuple(rows_of(midv, s, base + k) for k in range(3))

    def inside(s):
        there = brick > 0 if s == 0 else brick < bricks - 1
        return jnp.where(there, 1.0, 0.0).astype(jnp.float32)

    def order(s, f):
        return (f(-1), f(0), f(1)) if s == 0 else (f(1), f(0), f(-1))

    def fine(s, i, state, real):
        row = jnp.int32(i if s == 0 else n - 1 - i)
        turn = turning(row, brick * n, 1.0, all_rows, FINE_TIME)
        new = step(order(s, lambda d: state(i + d)), order(s, lambda d: depth(s, i + d)), wet(s, i), turn, FINE_TIME, 1)
        return scaled(new, real) if i < 0 else new

    def coarse(s, i, state, depths, wets, real):
        row = jnp.int32(i if s == 0 else m - 1 - i)
        turn = turning(row, brick * m, 2.0, all_rows, COARSE_TIME)
        new = step(order(s, lambda d: state(i + d)), order(s, lambda d: depths(i + d)), wets(i), turn, COARSE_TIME, 2)
        return scaled(new, real) if i < 0 else new

    def both(a, b):
        return tuple(average(x, y) for x, y in zip(a, b))

    def emit(s, i, rows):
        r = i if s == 0 else SUB - 1 - i
        for k in range(3):
            for j in range(nj):
                tiles[s, k, pl.ds(r + j * SUB, SUB, stride=nj * SUB), :] = rows[k][j]

    def flown(s, outer, real):
        one = {i: fine(s, i, lambda i: initial(s, i), real) for i in range(outer - 1, 1)}
        one.update({i: kept(s, MID_ONE + 3 * (i - 1)) for i in (1, 2)})
        return {i: fine(s, i, one.__getitem__, real) for i in range(outer, 2)}

    @pl.when(lane == 0)
    def _():
        for s in (0, 1):
            two = flown(s, 0, inside(s))
            for i in (0, 1):
                emit(s, i, two[i])

    @pl.when(lane != 0)
    def _():
        for s in (0, 1):
            real = inside(s)
            two = flown(s, -2, real)
            fresh = {i: both(two[2 * i], two[2 * i + 1]) for i in (-1, 0)}
            fresh.update({i: kept(s, MID_RF + 3 * (i - 1)) for i in (1, 2)})
            start = {i: both(initial(s, 2 * i), initial(s, 2 * i + 1)) for i in (-2, -1, 0, 1)}
            deep = {i: average(depth(s, 2 * i), depth(s, 2 * i + 1)) for i in range(-2, 3)}
            dry = {i: average(wet(s, 2 * i), wet(s, 2 * i + 1)) for i in (-1, 0, 1)}
            c1 = {i: coarse(s, i, start.__getitem__, deep.__getitem__, dry.__getitem__, real) for i in (-1, 0)}
            c1.update({i: kept(s, MID_C1 + 3 * (i - 1)) for i in (1, 2)})
            add = {}
            for i in (0, 1):
                x = coarse(s, i, fresh.__getitem__, deep.__getitem__, dry.__getitem__, real)
                y = coarse(s, i, c1.__getitem__, deep.__getitem__, dry.__getitem__, real)
                add[i] = [[a - b for a, b in zip(p, q)] for p, q in zip(x, y)]
            one = {i: fine(s, i, lambda i: c1[i // 2], real) for i in range(-1, 3)}
            one.update({i: kept(s, MID_PONE + 3 * (i - 3)) for i in (3, 4)})
            for i in range(4):
                rows = fine(s, i, one.__getitem__, real)
                emit(s, i, [[a + b for a, b in zip(x, y)] for x, y in zip(rows, add[i // 2])])

    back = [
        pltpu.make_async_copy(tiles.at[s], out.at[:, pl.ds(spots[s], tile), :], sems.at[2 + s])
        for s in (0, 1)
    ]
    for copy in back:
        copy.start()
    for copy in back:
        copy.wait()


def tiled(a):
    *lead, rows, cols = a.shape
    a = a.reshape(*lead, rows // SUB, SUB, cols // LANES, LANES)
    return jnp.swapaxes(a, -3, -2).reshape(*lead, rows * cols // LANES, LANES)


def untiled(a, rows, cols):
    lead = a.shape[:-2]
    a = a.reshape(*lead, rows // SUB, cols // LANES, SUB, LANES)
    return jnp.swapaxes(a, -3, -2).reshape(*lead, rows, cols)


def shards(initial, depth, mask):
    bricks = lax.axis_size("brick")
    n, cols = depth.shape
    nj = cols // (SUB * LANES)
    row = (nj, SUB, LANES)
    f32 = jnp.float32
    initial, depth, mask = tiled(initial), tiled(depth), tiled(mask)
    tile = nj * SUB * SUB
    size = depth.shape[0]
    params = pltpu.CompilerParams(vmem_limit_bytes=VMEM_LIMIT)
    anywhere = pl.BlockSpec(memory_space=pl.ANY)
    local = pl.BlockSpec(memory_space=pltpu.VMEM)

    packed = pl.pallas_call(
        functools.partial(pack_kernel, nj),
        out_shape=jax.ShapeDtypeStruct((PACKED, *row), f32),
        in_specs=[anywhere] * 3,
        out_specs=local,
        scratch_shapes=[
            pltpu.VMEM((3, tile, LANES), f32),
            pltpu.VMEM((tile, LANES), f32),
            pltpu.VMEM((tile, LANES), jnp.int32),
            pltpu.SemaphoreType.DMA((3,)),
        ],
        compiler_params=params,
        name="pack",
    )(initial, depth, mask)

    up = [(2 * i, 2 * i + 3) for i in range(bricks - 1)]
    down = [(2 * i + 3, 2 * i + 1) for i in range(bricks - 1)]
    low1 = lax.ppermute(packed, ("brick", "cuts"), up)
    high1 = lax.ppermute(packed, ("brick", "cuts"), down)
    low0 = lax.ppermute(low1, "cuts", [(1, 0)])
    high0 = lax.ppermute(high1, "cuts", [(1, 0)])

    out, mid = pl.pallas_call(
        functools.partial(middle_kernel, nj, bricks),
        out_shape=[jax.ShapeDtypeStruct((3, size, LANES), f32), jax.ShapeDtypeStruct((2, MID, *row), f32)],
        in_specs=[local] * 3,
        out_specs=[local] * 2,
        scratch_shapes=[
            pltpu.VMEM((n, 3, *row), f32),
            pltpu.VMEM((n, 2, *row), f32),
            pltpu.VMEM((n, 3, *row), f32),
            pltpu.VMEM((n, 3, *row), f32),
            pltpu.VMEM((n // 2, 3, *row), f32),
            pltpu.VMEM((n // 2, 2, *row), f32),
            pltpu.VMEM((n // 2, 3, *row), f32),
            pltpu.VMEM((n, 3, *row), f32),
            pltpu.VMEM((n // 2, 3, *row), f32),
        ],
        compiler_params=params,
        cost_estimate=pl.CostEstimate(flops=60 * 5 * n * cols, bytes_accessed=10 * n * cols * 4, transcendentals=0),
        name="middle",
    )(initial, depth, mask)

    out = pl.pallas_call(
        functools.partial(edge_kernel, nj, bricks, n),
        out_shape=jax.ShapeDtypeStruct((3, size, LANES), f32),
        in_specs=[anywhere] * 6,
        out_specs=anywhere,
        scratch_shapes=[
            pltpu.VMEM((2, PACKED, *row), f32),
            pltpu.VMEM((2, MID, *row), f32),
            pltpu.VMEM((2, 3, tile, LANES), f32),
            pltpu.SemaphoreType.DMA((6,)),
        ],
        input_output_aliases={5: 0},
        compiler_params=params,
        name="edges",
    )(low1, high1, low0, high0, mid, out)
    return untiled(out, n, cols)[None]


def solution(mesh):
    placed = (P(None, ("grp", "brick"), None), P("brick", None), P("brick", None))
    return jax.shard_map(
        shards,
        mesh=mesh,
        in_specs=placed,
        out_specs=P("cuts", None, ("grp", "brick"), None),
        check_vma=False,
    )
```

```python
import functools

import jax
import jax.numpy as jnp
from jax import lax
from jax.experimental import pallas as pl
from jax.experimental.pallas import tpu as pltpu
from jax.sharding import PartitionSpec as P


COURANT = 0.2
DIFFUSION = 0.05
FRICTION = 0.01
CORIOLIS = 0.5
FINE_TIME = 0.2
COARSE_TIME = 0.4
SUB, LANES = 8, 128
HALO = 4
PER = 5
PACKED = HALO * PER - 1
VMEM_LIMIT = 24 * 1024 * 1024


def next_col(x, amount, edge):
    turned = [pltpu.roll(a, LANES - amount, 1) for a in x]
    turned.append(pltpu.roll(turned[0], SUB - 1, 0))
    return [jnp.where(edge, turned[j + 1], turned[j]) for j in range(len(x))]


def prev_col(x, amount, edge):
    turned = [pltpu.roll(a, amount, 1) for a in x]
    turned.insert(0, pltpu.roll(turned[-1], 1, 0))
    return [jnp.where(edge, turned[j], turned[j + 1]) for j in range(len(x))]


def lane_ids():
    return lax.broadcasted_iota(jnp.int32, (SUB, LANES), 1)


def each(f, *rows):
    return [f(*a) for a in zip(*rows)]


def steps(states, heights, wets, turns, dt, cols, beside=None):
    lane = lane_ids()
    last, first = lane >= LANES - cols, lane < cols
    k = (1.0 - dt * FRICTION - 4.0 * DIFFUSION) / DIFFUSION
    full = [each(jnp.add, h, s[0]) for h, s in zip(heights, states)]
    flux = [each(jnp.multiply, f, s[1]) for f, s in zip(full, states)]
    out = []
    for i, (wet, t) in enumerate(zip(wets, turns)):
        (eb, ub, vb), (e, u, v), (ea, ua, va) = states[i : i + 3]
        e_r, e_l = next_col(e, cols, last), prev_col(e, cols, first)
        u_r, u_l = next_col(u, cols, last), prev_col(u, cols, first)
        v_r, v_l = next_col(v, cols, last), prev_col(v, cols, first)
        if beside is None:
            cross = each(jnp.multiply, full[i + 1], v)
            g_r, g_l = next_col(cross, cols, last), prev_col(cross, cols, first)
        else:
            g_r, g_l = (each(lambda h, a, b: (h + a) * b, *x) for x in zip(beside[i], (e_r, e_l), (v_r, v_l)))
        new_e, new_u, new_v = [], [], []
        for j in range(len(e)):
            spread = ((ea[j] - flux[i + 2][j]) + (eb[j] + flux[i][j])) + ((e_r[j] - g_r[j]) + (e_l[j] + g_l[j]))
            new_e.append(DIFFUSION * (e[j] * (1.0 / DIFFUSION - 4.0) + spread))
            nu = u[j] * (k - (ua[j] - ub[j])) + v[j] * (t - (u_r[j] - u_l[j]))
            nu = nu + (((ua[j] - ea[j]) + (ub[j] + eb[j])) + (u_r[j] + u_l[j]))
            nv = v[j] * (k - (v_r[j] - v_l[j])) - u[j] * (t + (va[j] - vb[j]))
            nv = nv + (((v_r[j] - e_r[j]) + (v_l[j] + e_l[j])) + (va[j] + vb[j]))
            new_u.append(nu * wet[j])
            new_v.append(nv * wet[j])
        out.append((new_e, new_u, new_v))
    return out


def average(low, high):
    even = lane_ids() % 2 == 0

    def one(a, b):
        s = a + b
        return (s + jnp.where(even, pltpu.roll(s, LANES - 1, 1), pltpu.roll(s, 1, 1))) * 0.25

    return each(one, low, high)


def average3(low, high):
    return tuple(average(a, b) for a, b in zip(low, high))


def interleave(x, y):
    even = lane_ids() % 2 == 0
    return tuple(each(lambda a, b: jnp.where(even, a, b), p, q) for p, q in zip(x, y))


def difference(z):
    even = lane_ids() % 2 == 0
    one = lambda a: jnp.where(even, a - pltpu.roll(a, LANES - 1, 1), pltpu.roll(a, 1, 1) - a)
    return tuple(each(one, row) for row in z)


def added(x, y):
    return tuple(each(jnp.add, a, b) for a, b in zip(x, y))


def rows_of(ref, *at):
    return [ref[(*at, j)] for j in range(ref.shape[-3])]


def put(ref, at, row):
    for j, a in enumerate(row):
        ref[(*at, j)] = a


def three(ref, at):
    return tuple(rows_of(ref, at, k) for k in range(3))


def put_three(ref, at, rows):
    for k, row in enumerate(rows):
        put(ref, (at, k), row)


def masked(rows, factor):
    e, u, v = rows
    return [a * factor for a in e], u, v


def turning(row, first_row, scale, all_rows, dt):
    y = (first_row + row).astype(jnp.float32) * (2.0 * scale) + scale
    return (dt * CORIOLIS / DIFFUSION) * (y * (1.0 / all_rows) - 1.0)


def in_tiles(nj, row, j):
    tile = nj * SUB * SUB
    return pl.ds((row // SUB) * tile + row % SUB + j * SUB, SUB, stride=nj * SUB)


SCALE = (4.0, 2.0, 2.0)


def emit(ref, at, nj, row, rows):
    for k in range(3):
        for j in range(nj):
            ref[(*at, k, in_tiles(nj, row, j))] = rows[k][j] * (1.0 / SCALE[k])


def wetness(mask):
    return mask.astype(jnp.float32) * DIFFUSION


def pack_kernel(nj, initial, depth, mask, out, initial_v, depth_v, mask_v, sems):
    lane = lax.axis_index("cuts")
    tile = nj * SUB * SUB
    high = initial.shape[1] // tile - 1
    start = pl.multiple_of(jnp.where(lane == 0, 0, high) * tile, tile)
    copies = [
        pltpu.make_async_copy(initial.at[:, pl.ds(start, tile), :], initial_v, sems.at[0]),
        pltpu.make_async_copy(depth.at[pl.ds(start, tile), :], depth_v, sems.at[1]),
        pltpu.make_async_copy(mask.at[pl.ds(start, tile), :], mask_v, sems.at[2]),
    ]
    for copy in copies:
        copy.start()
    for copy in copies:
        copy.wait()

    def fill(row_of):
        for d in range(HALO):
            for j in range(nj):
                at = in_tiles(nj, row_of(d), j)
                for k in range(3):
                    out[d * PER + k, j] = initial_v[k, at, :] * SCALE[k]
                out[d * PER + 3, j] = depth_v[at, :] * 4.0
                if d < HALO - 1:
                    out[d * PER + 4, j] = wetness(mask_v[at, :])

    pl.when(lane == 0)(lambda: fill(lambda d: d))
    pl.when(lane != 0)(lambda: fill(lambda d: SUB - 1 - d))


def loop(low, high, most, body):
    count = max(c for c in range(1, most + 1) if (high - low) % c == 0)

    def run(i, carry):
        body(low + i * count, count)
        return carry

    if high - low == count:
        body(low, count)
        return
    lax.fori_loop(0, (high - low) // count, run, 0)


def sideways(h):
    lane = lane_ids()
    return next_col(h, 1, lane >= LANES - 1), prev_col(h, 1, lane < 1)


def middle_kernel(nj, bricks, initial, depth, mask, out, ini, hw, s1, rc, c1, p1, tiles, s2, rhw, dif, sems):
    lane = lax.axis_index("cuts")
    brick = lax.axis_index("brick")
    n = ini.shape[0]
    m = n // 2
    all_rows = n * bricks
    tile = nj * SUB * SUB
    parts = n // SUB

    def load(t, carry):
        for r in range(SUB):
            row = t * SUB + r
            high = []
            for j in range(nj):
                at = pl.ds(t * tile + r + j * SUB, SUB, stride=nj * SUB)
                for k in range(3):
                    ini[row, k, j] = initial[k, at, :] * SCALE[k]
                high.append(depth[at, :] * 4.0)
                hw[row, 1, j] = wetness(mask[at, :])
            put(hw, (row, 0), high)
            for k, side in enumerate(sideways(high)):
                put(hw, (row, 2 + k), side)
        return carry

    lax.fori_loop(0, parts, load, 0)

    def fine(states, row, count):
        return steps(
            states,
            [rows_of(hw, row + d, 0) for d in range(-1, count + 1)],
            [rows_of(hw, row + d, 1) for d in range(count)],
            [turning(row + d, brick * n, 1.0, all_rows, FINE_TIME) for d in range(count)],
            FINE_TIME,
            1,
            [(rows_of(hw, row + d, 2), rows_of(hw, row + d, 3)) for d in range(count)],
        )

    def around(ref, row, count):
        return [three(ref, row + d) for d in range(-1, count + 1)]

    def coarse(states, row, count):
        return steps(
            states,
            [rows_of(rhw, row + d, 0) for d in range(-1, count + 1)],
            [rows_of(rhw, row + d, 1) for d in range(count)],
            [turning(row + d, brick * m, 2.0, all_rows, COARSE_TIME) for d in range(count)],
            COARSE_TIME,
            2,
        )

    def store(ref, row, new):
        for d, rows in enumerate(new):
            put_three(ref, row + d, rows)

    def send(t):
        at = pl.ds(t * tile, tile)
        return pltpu.make_async_copy(tiles.at[:, at, :], out.at[:, at, :], sems.at[t])

    def emitted(first, rows_at):
        for t in range(parts):
            low, high = max(first, t * SUB), min(n - first, (t + 1) * SUB)
            loop(low, high, 4, rows_at)
            send(t).start()
        for t in range(parts):
            send(t).wait()

    loop(1, n - 1, 5, lambda row, c: store(s1, row, fine(around(ini, row, c), row, c)))
    loop(2, n - 2, 4, lambda row, c: store(s2, row, fine(around(s1, row, c), row, c)))

    @pl.when(lane == 0)
    def _():
        def copied(row, count):
            for d in range(count):
                emit(tiles, (), nj, row + d, three(s2, row + d))

        emitted(2, copied)

    @pl.when(lane != 0)
    def _():
        def restrict(row, count):
            for d in range(count):
                low, high = 2 * (row + d), 2 * (row + d) + 1
                put_three(rc, row + d, average3(three(ini, low), three(ini, high)))
                for k in range(2):
                    put(rhw, (row + d, k), average(rows_of(hw, low, k), rows_of(hw, high, k)))

        loop(0, m, 4, restrict)
        loop(1, m - 1, 7, lambda row, c: store(c1, row, coarse(around(rc, row, c), row, c)))

        def again(row, count):
            for d in range(count):
                low, high = 2 * (row + d), 2 * (row + d) + 1
                put_three(rc, row + d, average3(three(s2, low), three(s2, high)))

        loop(1, m - 1, 7, again)

        def correct(row, count):
            both = [interleave(a, b) for a, b in zip(around(rc, row, count), around(c1, row, count))]
            store(dif, row, [difference(z) for z in coarse(both, row, count)])

        loop(2, m - 2, 4, correct)

        def prolonged(half, count):
            row = 2 * half + 1
            pairs = [three(c1, half + d) for d in range(count + 1)]
            store(p1, row, fine([pairs[d // 2] for d in range(2 * count + 2)], row, 2 * count))

        loop(1, m - 2, 2, prolonged)

        def last(row, count):
            for d, rows in enumerate(fine(around(p1, row, count), row, count)):
                emit(tiles, (), nj, row + d, added(rows, three(dif, (row + d) // 2)))

        emitted(4, last)


def edge_kernel(nj, bricks, n, turned, near, ini, hw, s1, rf, c1, p1, before, out, tiles, sems):
    lane = lax.axis_index("cuts")
    brick = lax.axis_index("brick")
    all_rows = n * bricks
    m = n // 2
    wide = nj * SUB

    def own(s, i, count):
        return i if s == 0 else count - 1 - i

    def depth(s, i):
        return rows_of(near, (-1 - i) * PER + 3) if i < 0 else rows_of(hw, own(s, i, n), 0)

    def wet(s, i):
        return rows_of(near, (-1 - i) * PER + 4) if i < 0 else rows_of(hw, own(s, i, n), 1)

    def initial(s, i):
        if i < 0:
            return tuple(rows_of(near, (-1 - i) * PER + k) for k in range(3))
        return three(ini, own(s, i, n))

    def known(ref, s, ids):
        return {i: three(ref, own(s, i, ref.shape[0])) for i in ids}

    def inside(s):
        there = brick > 0 if s == 0 else brick < bricks - 1
        return jnp.where(there, 1.0, 0.0).astype(jnp.float32)

    def advance(s, ids, state, heights, wets, turn, dt, cols, beside=None):
        run = list(ids) if s == 0 else list(ids)[::-1]
        way = 1 if s == 0 else -1
        span = [run[0] - way, *run, run[-1] + way]
        sides = None if beside is None else [beside(i) for i in run]
        new = steps([state(i) for i in span], [heights(i) for i in span], [wets(i) for i in run], [turn(i) for i in run], dt, cols, sides)
        return {i: masked(x, inside(s)) if i < 0 else x for i, x in zip(run, new)}

    def fine(s, ids, state, beside):
        turn = lambda i: turning(jnp.int32(own(s, i, n)), brick * n, 1.0, all_rows, FINE_TIME)
        return advance(s, ids, state, lambda i: depth(s, i), lambda i: wet(s, i), turn, FINE_TIME, 1, beside)

    def coarse(s, ids, state, deep, dry):
        turn = lambda i: turning(jnp.int32(own(s, i, m)), brick * m, 2.0, all_rows, COARSE_TIME)
        return advance(s, ids, state, deep.__getitem__, dry.__getitem__, turn, COARSE_TIME, 2)

    def sides_from(s, outer):
        held = {i: sideways(depth(s, i)) for i in range(outer, 0)}
        return lambda i: held[i] if i < 0 else (rows_of(hw, own(s, i, n), 2), rows_of(hw, own(s, i, n), 3))

    def flown(s, outer, beside):
        one = fine(s, range(outer - 1, 1), lambda i: initial(s, i), beside)
        one.update(known(s1, s, (1, 2)))
        return fine(s, range(outer, 2), one.__getitem__, beside)

    def send(s, rows):
        count = len(rows)
        for i, x in rows.items():
            emit(tiles, (), nj, own(s, i, SUB), x)
        at = 0 if s == 0 else SUB - count
        where = 0 if s == 0 else (n // SUB - 1) * wide
        src = tiles.reshape(3, wide, SUB, LANES).at[:, :, at : at + count, :]
        copy = pltpu.make_async_copy(src, out.at[:, where : where + wide, at : at + count, :], sems.at[0])
        copy.start()
        copy.wait()

    @pl.when(lane == 0)
    def _():
        s = int(turned)
        send(s, {i: x for i, x in flown(s, 0, sides_from(s, -1)).items() if i >= 0})

    @pl.when(lane != 0)
    def _():
        s = 1 - int(turned)
        beside = sides_from(s, -3)
        two = flown(s, -2, beside)
        fresh = {i: average3(two[2 * i], two[2 * i + 1]) for i in (-1, 0)}
        fresh.update(known(rf, s, (1, 2)))
        start = {i: average3(initial(s, 2 * i), initial(s, 2 * i + 1)) for i in range(-2, 2)}
        deep = {i: average(depth(s, 2 * i), depth(s, 2 * i + 1)) for i in range(-2, 3)}
        dry = {i: average(wet(s, 2 * i), wet(s, 2 * i + 1)) for i in (-1, 0, 1)}
        first = coarse(s, (-1, 0), start.__getitem__, deep, dry)
        first.update(known(c1, s, (1, 2)))
        both = {i: interleave(fresh[i], first[i]) for i in range(-1, 3)}
        add = {i: difference(z) for i, z in coarse(s, (0, 1), both.__getitem__, deep, dry).items()}
        one = fine(s, range(-1, 3), lambda i: first[i // 2], beside)
        one.update(known(p1, s, (3, 4)))
        send(s, {i: added(x, add[i // 2]) for i, x in fine(s, range(4), one.__getitem__, beside).items()})


def tiled(a):
    *lead, rows, cols = a.shape
    a = a.reshape(*lead, rows // SUB, SUB, cols // LANES, LANES)
    return jnp.swapaxes(a, -3, -2).reshape(*lead, rows * cols // LANES, LANES)


def untiled(a, rows, cols):
    lead = a.shape[:-2]
    a = a.reshape(*lead, rows // SUB, cols // LANES, SUB, LANES)
    return jnp.swapaxes(a, -3, -2).reshape(*lead, rows, cols)


def shards(initial, depth, mask):
    bricks = lax.axis_size("brick")
    n, cols = depth.shape
    nj = cols // (SUB * LANES)
    row = (nj, SUB, LANES)
    f32 = jnp.float32
    initial, depth, mask = tiled(initial), tiled(depth), tiled(mask)
    tile = nj * SUB * SUB
    size = depth.shape[0]
    params = pltpu.CompilerParams(vmem_limit_bytes=VMEM_LIMIT)
    far = pl.BlockSpec(memory_space=pltpu.HBM)
    local = pl.BlockSpec(memory_space=pltpu.VMEM)

    def hold(rows, count):
        return jax.ShapeDtypeStruct((rows, count, *row), f32)

    packed = pl.pallas_call(
        functools.partial(pack_kernel, nj),
        out_shape=jax.ShapeDtypeStruct((PACKED, *row), f32),
        in_specs=[far] * 3,
        out_specs=local,
        scratch_shapes=[
            pltpu.VMEM((3, tile, LANES), f32),
            pltpu.VMEM((tile, LANES), f32),
            pltpu.VMEM((tile, LANES), jnp.int32),
            pltpu.SemaphoreType.DMA((3,)),
        ],
        compiler_params=params,
        name="pack",
    )(*(pltpu.with_memory_space_constraint(a, pltpu.HBM) for a in (initial, depth, mask)))

    up = [(2 * i + 1, 2 * i + 2) for i in range(bricks - 1)]
    near = lax.ppermute(packed, ("brick", "cuts"), up + [(b, a) for a, b in up])

    whole, *held = pl.pallas_call(
        functools.partial(middle_kernel, nj, bricks),
        out_shape=[
            jax.ShapeDtypeStruct((3, size, LANES), f32),
            hold(n, 3),
            hold(n, 4),
            hold(n, 3),
            hold(n // 2, 3),
            hold(n // 2, 3),
            hold(n, 3),
        ],
        in_specs=[local] * 3,
        out_specs=[far] + [local] * 6,
        scratch_shapes=[
            pltpu.VMEM((3, size, LANES), f32),
            pltpu.VMEM((n, 3, *row), f32),
            pltpu.VMEM((n // 2, 2, *row), f32),
            pltpu.VMEM((n // 2, 3, *row), f32),
            pltpu.SemaphoreType.DMA((n // SUB,)),
        ],
        compiler_params=params,
        cost_estimate=pl.CostEstimate(flops=60 * 5 * n * cols, bytes_accessed=10 * n * cols * 4, transcendentals=0),
        name="middle",
    )(initial, depth, mask)

    def edges(turned, near, before):
        return pl.pallas_call(
            functools.partial(edge_kernel, nj, bricks, n, turned),
            out_shape=jax.ShapeDtypeStruct((3, size // SUB, SUB, LANES), f32),
            in_specs=[local] * 7 + [far],
            out_specs=far,
            scratch_shapes=[pltpu.VMEM((3, tile, LANES), f32), pltpu.SemaphoreType.DMA((1,))],
            input_output_aliases={7: 0},
            compiler_params=params,
            cost_estimate=pl.CostEstimate(flops=60 * n * cols, bytes_accessed=n * cols * 4, transcendentals=0),
            name="edges",
        )(near, *held, before)

    near, *held = lax.optimization_barrier((near, *held))
    other = lax.ppermute(near, "cuts", [(0, 1), (1, 0)])
    whole = edges(False, near, whole.reshape(3, size // SUB, SUB, LANES))
    whole = edges(True, other, whole)
    return untiled(whole.reshape(3, size, LANES), n, cols)[None]


def solution(mesh):
    placed = (P(None, ("grp", "brick"), None), P("brick", None), P("brick", None))
    return jax.shard_map(
        shards,
        mesh=mesh,
        in_specs=placed,
        out_specs=P("cuts", None, ("grp", "brick"), None),
        check_vma=False,
    )
```

```python
import functools

import jax
import jax.numpy as jnp
from jax import lax
from jax.experimental import pallas as pl
from jax.experimental.pallas import tpu as pltpu
from jax.sharding import PartitionSpec as P


COURANT = 0.2
DIFFUSION = 0.05
FRICTION = 0.01
CORIOLIS = 0.5
FINE_TIME = 0.2
COARSE_TIME = 0.4
SUB, LANES = 8, 128
HALO = 4
PER = 5
PACKED = HALO * PER - 1
VMEM_LIMIT = 24 * 1024 * 1024


def next_col(x, amount, edge):
    turned = [pltpu.roll(a, LANES - amount, 1) for a in x]
    turned.append(pltpu.roll(turned[0], SUB - 1, 0))
    return [jnp.where(edge, turned[j + 1], turned[j]) for j in range(len(x))]


def prev_col(x, amount, edge):
    turned = [pltpu.roll(a, amount, 1) for a in x]
    turned.insert(0, pltpu.roll(turned[-1], 1, 0))
    return [jnp.where(edge, turned[j], turned[j + 1]) for j in range(len(x))]


def lane_ids():
    return lax.broadcasted_iota(jnp.int32, (SUB, LANES), 1)


def each(f, *rows):
    return [f(*a) for a in zip(*rows)]


def steps(states, heights, wets, turns, dt, cols, beside):
    lane = lane_ids()
    last, first = lane >= LANES - cols, lane < cols
    k = (1.0 - dt * FRICTION - 4.0 * DIFFUSION) / DIFFUSION
    full = [each(jnp.add, h, s[0]) for h, s in zip(heights, states)]
    flux = [each(jnp.multiply, f, s[1]) for f, s in zip(full, states)]
    out = []
    shifted = None
    for i, (wet, t) in enumerate(zip(wets, turns)):
        (eb, ub, vb), (e, u, v), (ea, ua, va) = states[i : i + 3]
        if shifted is None or states[i + 1] is not states[i]:
            shifted = [(next_col(a, cols, last), prev_col(a, cols, first)) for a in (e, u, v)]
        (e_r, e_l), (u_r, u_l), (v_r, v_l) = shifted
        g_r, g_l = (each(lambda h, a, b: (h + a) * b, *x) for x in zip(beside[i], (e_r, e_l), (v_r, v_l)))
        new_e, new_u, new_v = [], [], []
        for j in range(len(e)):
            spread = ((ea[j] - flux[i + 2][j]) + (eb[j] + flux[i][j])) + ((e_r[j] - g_r[j]) + (e_l[j] + g_l[j]))
            new_e.append(DIFFUSION * (e[j] * (1.0 / DIFFUSION - 4.0) + spread))
            nu = u[j] * (k - (ua[j] - ub[j])) + v[j] * (t - (u_r[j] - u_l[j]))
            nu = nu + (((ua[j] - ea[j]) + (ub[j] + eb[j])) + (u_r[j] + u_l[j]))
            nv = v[j] * (k - (v_r[j] - v_l[j])) - u[j] * (t + (va[j] - vb[j]))
            nv = nv + (((v_r[j] - e_r[j]) + (v_l[j] + e_l[j])) + (va[j] + vb[j]))
            new_u.append(nu * wet[j])
            new_v.append(nv * wet[j])
        out.append((new_e, new_u, new_v))
    return out


def average(low, high):
    even = lane_ids() % 2 == 0

    def one(a, b):
        s = a + b
        return (s + jnp.where(even, pltpu.roll(s, LANES - 1, 1), pltpu.roll(s, 1, 1))) * 0.25

    return each(one, low, high)


def average3(low, high):
    return tuple(average(a, b) for a, b in zip(low, high))


def interleave(x, y):
    even = lane_ids() % 2 == 0
    return tuple(each(lambda a, b: jnp.where(even, a, b), p, q) for p, q in zip(x, y))


def difference(z):
    even = lane_ids() % 2 == 0
    one = lambda a: jnp.where(even, a - pltpu.roll(a, LANES - 1, 1), pltpu.roll(a, 1, 1) - a)
    return tuple(each(one, row) for row in z)


def added(x, y):
    return tuple(each(jnp.add, a, b) for a, b in zip(x, y))


def rows_of(ref, *at):
    return [ref[(*at, j)] for j in range(ref.shape[-3])]


def put(ref, at, row):
    for j, a in enumerate(row):
        ref[(*at, j)] = a


def three(ref, at):
    return tuple(rows_of(ref, at, k) for k in range(3))


def put_three(ref, at, rows):
    for k, row in enumerate(rows):
        put(ref, (at, k), row)


def masked(rows, factor):
    e, u, v = rows
    return [a * factor for a in e], u, v


def turning(row, first_row, scale, all_rows, dt):
    y = (first_row + row).astype(jnp.float32) * (2.0 * scale) + scale
    return (dt * CORIOLIS / DIFFUSION) * (y * (1.0 / all_rows) - 1.0)


def in_tiles(nj, row, j):
    tile = nj * SUB * SUB
    return pl.ds((row // SUB) * tile + row % SUB + j * SUB, SUB, stride=nj * SUB)


SCALE = (4.0, 2.0, 2.0)


def emit(ref, at, nj, row, rows):
    for k in range(3):
        for j in range(nj):
            ref[(*at, k, in_tiles(nj, row, j))] = rows[k][j] * (1.0 / SCALE[k])


def wetness(mask):
    return mask.astype(jnp.float32) * DIFFUSION


def pack_kernel(nj, initial, depth, mask, out, initial_v, depth_v, mask_v, sems):
    lane = lax.axis_index("cuts")
    wide = nj * SUB

    def fill(tile, at, row_of):
        there = pl.ds(tile, wide), pl.ds(at, HALO)
        copies = [
            pltpu.make_async_copy(initial.at[:, *there, :], initial_v, sems.at[0]),
            pltpu.make_async_copy(depth.at[*there, :], depth_v, sems.at[1]),
            pltpu.make_async_copy(mask.at[*there, :], mask_v, sems.at[2]),
        ]
        for copy in copies:
            copy.start()
        for copy in copies:
            copy.wait()
        flat = [ref.reshape(*ref.shape[:-3], wide * HALO, LANES) for ref in (initial_v, depth_v, mask_v)]
        for d in range(HALO):
            for j in range(nj):
                at = pl.ds(row_of(d) + j * HALO, SUB, stride=nj * HALO)
                for k in range(3):
                    out[d * PER + k, j] = flat[0][k, at, :] * SCALE[k]
                out[d * PER + 3, j] = flat[1][at, :] * 4.0
                if d < HALO - 1:
                    out[d * PER + 4, j] = wetness(flat[2][at, :])

    pl.when(lane == 0)(lambda: fill(0, 0, lambda d: d))
    pl.when(lane != 0)(lambda: fill(depth.shape[0] - wide, SUB - HALO, lambda d: HALO - 1 - d))


def loop(low, high, count, body):
    times, rest = divmod(high - low, count)

    def run(i, carry):
        body(low + i * count, count)
        return carry

    if times > 1:
        lax.fori_loop(0, times, run, 0)
    elif times:
        body(low, count)
    if rest:
        body(high - rest, rest)


def sideways(h, cols):
    lane = lane_ids()
    return next_col(h, cols, lane >= LANES - cols), prev_col(h, cols, lane < cols)


def middle_kernel(nj, bricks, initial, depth, mask, tiles, ini, hw, s1, rc, rhw, rf, c1, p1, s2, dif):
    lane = lax.axis_index("cuts")
    brick = lax.axis_index("brick")
    n = ini.shape[0]
    m = n // 2
    all_rows = n * bricks
    tile = nj * SUB * SUB
    parts = n // SUB

    def load(t, carry):
        for r in range(SUB):
            row = t * SUB + r
            high = []
            for j in range(nj):
                at = pl.ds(t * tile + r + j * SUB, SUB, stride=nj * SUB)
                for k in range(3):
                    ini[row, k, j] = initial[k, at, :] * SCALE[k]
                high.append(depth[at, :] * 4.0)
                hw[row, 1, j] = wetness(mask[at, :])
            put(hw, (row, 0), high)
            for k, side in enumerate(sideways(high, 1)):
                put(hw, (row, 2 + k), side)
        return carry

    lax.fori_loop(0, parts, load, 0)

    def fine(states, row, count):
        return steps(
            states,
            [rows_of(hw, row + d, 0) for d in range(-1, count + 1)],
            [rows_of(hw, row + d, 1) for d in range(count)],
            [turning(row + d, brick * n, 1.0, all_rows, FINE_TIME) for d in range(count)],
            FINE_TIME,
            1,
            [(rows_of(hw, row + d, 2), rows_of(hw, row + d, 3)) for d in range(count)],
        )

    def around(ref, row, count):
        return [three(ref, row + d) for d in range(-1, count + 1)]

    def coarse(states, row, count):
        return steps(
            states,
            [rows_of(rhw, row + d, 0) for d in range(-1, count + 1)],
            [rows_of(rhw, row + d, 1) for d in range(count)],
            [turning(row + d, brick * m, 2.0, all_rows, COARSE_TIME) for d in range(count)],
            COARSE_TIME,
            2,
            [(rows_of(rhw, row + d, 2), rows_of(rhw, row + d, 3)) for d in range(count)],
        )

    def store(ref, row, new):
        for d, rows in enumerate(new):
            put_three(ref, row + d, rows)

    loop(1, n - 1, n - 2, lambda row, c: store(s1, row, fine(around(ini, row, c), row, c)))
    loop(2, n - 2, n - 4, lambda row, c: store(s2, row, fine(around(s1, row, c), row, c)))

    @pl.when(lane == 0)
    def _():
        def copied(row, count):
            for d in range(count):
                emit(tiles, (), nj, row + d, three(s2, row + d))

        loop(2, n - 2, 4, copied)

    @pl.when(lane != 0)
    def _():
        def restrict(row, count):
            for d in range(count):
                low, high = 2 * (row + d), 2 * (row + d) + 1
                put_three(rc, row + d, average3(three(ini, low), three(ini, high)))

        def restrict_depth(row, count):
            for d in range(count):
                low, high = 2 * (row + d), 2 * (row + d) + 1
                deep = average(rows_of(hw, low, 0), rows_of(hw, high, 0))
                dry = average(rows_of(hw, low, 1), rows_of(hw, high, 1))
                for k, x in enumerate((deep, dry, *sideways(deep, 2))):
                    put(rhw, (row + d, k), x)

        loop(0, m, 4, restrict)
        loop(0, m, 4, restrict_depth)
        loop(1, m - 1, m - 2, lambda row, c: store(c1, row, coarse(around(rc, row, c), row, c)))

        def again(row, count):
            for d in range(count):
                low, high = 2 * (row + d), 2 * (row + d) + 1
                put_three(rf, row + d, average3(three(s2, low), three(s2, high)))

        loop(1, m - 1, m - 2, again)

        def correct(row, count):
            both = [interleave(a, b) for a, b in zip(around(rf, row, count), around(c1, row, count))]
            store(dif, row, [difference(z) for z in coarse(both, row, count)])

        loop(2, m - 2, m - 4, correct)

        def prolonged(half, count):
            pairs = around(c1, half, count)
            twice = [pairs[(d + 1) // 2] for d in range(2 * count + 2)]
            store(p1, 2 * half, fine(twice, 2 * half, 2 * count))

        loop(2, m - 2, m - 4, prolonged)
        for row in (3, n - 4):
            store(p1, row, fine([three(c1, (row + d) // 2) for d in (-1, 0, 1)], row, 1))

        def last(row, count):
            for d, rows in enumerate(fine(around(p1, row, count), row, count)):
                emit(tiles, (), nj, row + d, added(rows, three(dif, (row + d) // 2)))

        loop(4, n - 4, n - 8, last)


def edge_kernel(nj, bricks, n, turned, near, ini, hw, s1, rc, rhw, rf, c1, p1, *refs):
    lane = lax.axis_index("cuts")
    brick = lax.axis_index("brick")
    all_rows = n * bricks
    m = n // 2
    wide = nj * SUB
    if turned:
        ready, _, out, tiles, sems = refs
    else:
        middle, out, tiles, sems = refs

    def own(s, i, count):
        return i if s == 0 else count - 1 - i

    def depth(s, i):
        return rows_of(near, (-1 - i) * PER + 3) if i < 0 else rows_of(hw, own(s, i, n), 0)

    def wet(s, i):
        return rows_of(near, (-1 - i) * PER + 4) if i < 0 else rows_of(hw, own(s, i, n), 1)

    def initial(s, i):
        if i < 0:
            return tuple(rows_of(near, (-1 - i) * PER + k) for k in range(3))
        return three(ini, own(s, i, n))

    def known(ref, s, ids):
        return {i: three(ref, own(s, i, ref.shape[0])) for i in ids}

    def inside(s):
        there = brick > 0 if s == 0 else brick < bricks - 1
        return jnp.where(there, 1.0, 0.0).astype(jnp.float32)

    def advance(s, ids, state, heights, wets, turn, dt, cols, beside):
        run = list(ids) if s == 0 else list(ids)[::-1]
        way = 1 if s == 0 else -1
        span = [run[0] - way, *run, run[-1] + way]
        sides = [beside(i) for i in run]
        new = steps([state(i) for i in span], [heights(i) for i in span], [wets(i) for i in run], [turn(i) for i in run], dt, cols, sides)
        return {i: masked(x, inside(s)) if i < 0 else x for i, x in zip(run, new)}

    def fine(s, ids, state, beside):
        turn = lambda i: turning(jnp.int32(own(s, i, n)), brick * n, 1.0, all_rows, FINE_TIME)
        return advance(s, ids, state, lambda i: depth(s, i), lambda i: wet(s, i), turn, FINE_TIME, 1, beside)

    def coarse(s, ids, state, deep, dry, beside):
        turn = lambda i: turning(jnp.int32(own(s, i, m)), brick * m, 2.0, all_rows, COARSE_TIME)
        return advance(s, ids, state, deep.__getitem__, dry.__getitem__, turn, COARSE_TIME, 2, beside.__getitem__)

    def sides_from(s, outer):
        held = {i: sideways(depth(s, i), 1) for i in range(outer, 0)}
        return lambda i: held[i] if i < 0 else (rows_of(hw, own(s, i, n), 2), rows_of(hw, own(s, i, n), 3))

    def flown(s, outer, beside):
        start = {i: initial(s, i) for i in range(outer - 2, 2)}
        one = fine(s, range(outer - 1, 1), start.__getitem__, beside)
        one.update(known(s1, s, (1, 2)))
        return fine(s, range(outer, 2), one.__getitem__, beside)

    def sent(ref, s, count, sem):
        at = 0 if s == 0 else SUB - count
        where = 0 if s == 0 else (n // SUB - 1) * wide
        src = ref.reshape(3, wide, SUB, LANES).at[:, :, at : at + count, :]
        return pltpu.make_async_copy(src, out.at[:, where : where + wide, at : at + count, :], sems.at[sem])

    def earlier(s, count):
        return sent(ready, 1 - s, count, 0) if turned else pltpu.make_async_copy(middle, out, sems.at[0])

    def finished(s, count, rows_of_side):
        for i, x in rows_of_side().items():
            if i >= 0:
                emit(tiles, (), nj, own(s, i, SUB), x)
        if turned:
            later = sent(tiles, s, count, 1)
            later.start()
            later.wait()
        earlier(s, count).wait()

    def first_end(s):
        return flown(s, 0, sides_from(s, -1))

    def second_end(s):
        beside = sides_from(s, -3)
        two = flown(s, -2, beside)
        fresh = {i: average3(two[2 * i], two[2 * i + 1]) for i in (-1, 0)}
        fresh.update(known(rf, s, (1, 2)))
        start = {i: average3(initial(s, 2 * i), initial(s, 2 * i + 1)) for i in (-2, -1)}
        start.update(known(rc, s, (0, 1)))
        deep = {i: average(depth(s, 2 * i), depth(s, 2 * i + 1)) for i in (-2, -1)}
        deep.update({i: rows_of(rhw, own(s, i, m), 0) for i in (0, 1, 2)})
        dry = {-1: average(wet(s, -2), wet(s, -1))}
        dry.update({i: rows_of(rhw, own(s, i, m), 1) for i in (0, 1)})
        aside = {-1: sideways(deep[-1], 2)}
        aside.update({i: (rows_of(rhw, own(s, i, m), 2), rows_of(rhw, own(s, i, m), 3)) for i in (0, 1)})
        first = coarse(s, (-1, 0), start.__getitem__, deep, dry, aside)
        first.update(known(c1, s, (1, 2)))
        both = {i: interleave(fresh[i], first[i]) for i in range(-1, 3)}
        add = {i: difference(z) for i, z in coarse(s, (0, 1), both.__getitem__, deep, dry, aside).items()}
        one = fine(s, range(-1, 3), lambda i: first[i // 2], beside)
        one.update(known(p1, s, (3, 4)))
        return {i: added(x, add[i // 2]) for i, x in fine(s, range(4), one.__getitem__, beside).items()}

    one, two = int(turned), 1 - int(turned)
    pl.when(lane == 0)(lambda: earlier(one, 2).start())
    pl.when(lane != 0)(lambda: earlier(two, 4).start())
    pl.when(lane == 0)(lambda: finished(one, 2, lambda: first_end(one)))
    pl.when(lane != 0)(lambda: finished(two, 4, lambda: second_end(two)))


def tiled(a):
    *lead, rows, cols = a.shape
    a = a.reshape(*lead, rows // SUB, SUB, cols // LANES, LANES)
    return jnp.swapaxes(a, -3, -2).reshape(*lead, rows * cols // LANES, LANES)


def untiled(a, rows, cols):
    lead = a.shape[:-2]
    a = a.reshape(*lead, rows // SUB, cols // LANES, SUB, LANES)
    return jnp.swapaxes(a, -3, -2).reshape(*lead, rows, cols)


def shards(initial, depth, mask):
    bricks = lax.axis_size("brick")
    n, cols = depth.shape
    nj = cols // (SUB * LANES)
    row = (nj, SUB, LANES)
    f32 = jnp.float32
    initial, depth, mask = tiled(initial), tiled(depth), tiled(mask)
    tile = nj * SUB * SUB
    size = depth.shape[0]
    params = pltpu.CompilerParams(vmem_limit_bytes=VMEM_LIMIT)
    far = pl.BlockSpec(memory_space=pltpu.HBM)
    local = pl.BlockSpec(memory_space=pltpu.VMEM)

    def hold(rows, count):
        return jax.ShapeDtypeStruct((rows, count, *row), f32)

    def rows8(a):
        return a.reshape(*a.shape[:-2], -1, SUB, LANES)

    wide = nj * SUB
    packed = pl.pallas_call(
        functools.partial(pack_kernel, nj),
        out_shape=jax.ShapeDtypeStruct((PACKED, *row), f32),
        in_specs=[far] * 3,
        out_specs=local,
        scratch_shapes=[
            pltpu.VMEM((3, wide, HALO, LANES), f32),
            pltpu.VMEM((wide, HALO, LANES), f32),
            pltpu.VMEM((wide, HALO, LANES), jnp.int32),
            pltpu.SemaphoreType.DMA((3,)),
        ],
        compiler_params=params,
        name="pack",
    )(*(pltpu.with_memory_space_constraint(rows8(a), pltpu.HBM) for a in (initial, depth, mask)))
    packed, initial, depth, mask = lax.optimization_barrier((packed, initial, depth, mask))

    up = [(2 * i + 1, 2 * i + 2) for i in range(bricks - 1)]
    near = lax.ppermute(packed, ("brick", "cuts"), up + [(b, a) for a, b in up])

    inner, *held = pl.pallas_call(
        functools.partial(middle_kernel, nj, bricks),
        out_shape=[
            jax.ShapeDtypeStruct((3, size, LANES), f32),
            hold(n, 3),
            hold(n, 4),
            hold(n, 3),
            hold(n // 2, 3),
            hold(n // 2, 4),
            hold(n // 2, 3),
            hold(n // 2, 3),
            hold(n, 3),
        ],
        in_specs=[local] * 3,
        out_specs=[local] * 9,
        scratch_shapes=[
            pltpu.VMEM((n, 3, *row), f32),
            pltpu.VMEM((n // 2, 3, *row), f32),
        ],
        compiler_params=params,
        cost_estimate=pl.CostEstimate(flops=60 * 5 * n * cols, bytes_accessed=10 * n * cols * 4, transcendentals=0),
        name="middle",
    )(initial, depth, mask)

    def edges(turned, near, *more):
        result = jax.ShapeDtypeStruct((3, size // SUB, SUB, LANES), f32)
        part = jax.ShapeDtypeStruct((3, tile, LANES), f32)
        return pl.pallas_call(
            functools.partial(edge_kernel, nj, bricks, n, turned),
            out_shape=result if turned else [result, part],
            in_specs=[local] * 10 + ([far] if turned else []),
            out_specs=far if turned else [far, local],
            scratch_shapes=[pltpu.VMEM(part.shape, f32)] * turned + [pltpu.SemaphoreType.DMA((2,))],
            input_output_aliases={10: 0} if turned else {},
            compiler_params=params,
            cost_estimate=pl.CostEstimate(flops=60 * n * cols, bytes_accessed=n * cols * 4, transcendentals=0),
            name="edges",
        )(near, *held, *more)

    near, inner, *held = lax.optimization_barrier((near, inner, *held))
    other = lax.ppermute(near, "cuts", [(0, 1), (1, 0)])
    whole, ready = edges(False, near, rows8(inner))
    whole = edges(True, other, ready, whole)
    return untiled(whole.reshape(3, size, LANES), n, cols)[None]


def solution(mesh):
    placed = (P(None, ("grp", "brick"), None), P("brick", None), P("brick", None))
    return jax.shard_map(
        shards,
        mesh=mesh,
        in_specs=placed,
        out_specs=P("cuts", None, ("grp", "brick"), None),
        check_vma=False,
    )
```

```python
import functools

import jax
import jax.numpy as jnp
from jax import lax
from jax.experimental import pallas as pl
from jax.experimental.pallas import tpu as pltpu
from jax.sharding import PartitionSpec as P


COURANT = 0.2
DIFFUSION = 0.05
FRICTION = 0.01
CORIOLIS = 0.5
FINE_TIME = 0.2
COARSE_TIME = 0.4
SUB, LANES = 8, 128
HALO = 4
PER = 5
PACKED = HALO * PER - 1
VMEM_LIMIT = 24 * 1024 * 1024


def next_col(x, amount, edge):
    turned = [pltpu.roll(a, LANES - amount, 1) for a in x]
    turned.append(pltpu.roll(turned[0], SUB - 1, 0))
    return [jnp.where(edge, turned[j + 1], turned[j]) for j in range(len(x))]


def prev_col(x, amount, edge):
    turned = [pltpu.roll(a, amount, 1) for a in x]
    turned.insert(0, pltpu.roll(turned[-1], 1, 0))
    return [jnp.where(edge, turned[j], turned[j + 1]) for j in range(len(x))]


def lane_ids():
    return lax.broadcasted_iota(jnp.int32, (SUB, LANES), 1)


def each(f, *rows):
    return [f(*a) for a in zip(*rows)]


def steps(states, heights, wets, turns, dt, cols, beside):
    lane = lane_ids()
    last, first = lane >= LANES - cols, lane < cols
    k = (1.0 - dt * FRICTION - 4.0 * DIFFUSION) / DIFFUSION
    full = [each(jnp.add, h, s[0]) for h, s in zip(heights, states)]
    flux = [each(jnp.multiply, f, s[1]) for f, s in zip(full, states)]
    out = []
    shifted = None
    for i, (wet, t) in enumerate(zip(wets, turns)):
        (eb, ub, vb), (e, u, v), (ea, ua, va) = states[i : i + 3]
        if shifted is None or states[i + 1] is not states[i]:
            shifted = [(next_col(a, cols, last), prev_col(a, cols, first)) for a in (e, u, v)]
        (e_r, e_l), (u_r, u_l), (v_r, v_l) = shifted
        g_r, g_l = (each(lambda h, a, b: (h + a) * b, *x) for x in zip(beside[i], (e_r, e_l), (v_r, v_l)))
        new_e, new_u, new_v = [], [], []
        for j in range(len(e)):
            spread = ((ea[j] - flux[i + 2][j]) + (eb[j] + flux[i][j])) + ((e_r[j] - g_r[j]) + (e_l[j] + g_l[j]))
            new_e.append(DIFFUSION * (e[j] * (1.0 / DIFFUSION - 4.0) + spread))
            nu = u[j] * (k - (ua[j] - ub[j])) + v[j] * (t - (u_r[j] - u_l[j]))
            nu = nu + (((ua[j] - ea[j]) + (ub[j] + eb[j])) + (u_r[j] + u_l[j]))
            nv = v[j] * (k - (v_r[j] - v_l[j])) - u[j] * (t + (va[j] - vb[j]))
            nv = nv + (((v_r[j] - e_r[j]) + (v_l[j] + e_l[j])) + (va[j] + vb[j]))
            new_u.append(nu * wet[j])
            new_v.append(nv * wet[j])
        out.append((new_e, new_u, new_v))
    return out


def average(low, high):
    even = lane_ids() % 2 == 0

    def one(a, b):
        s = a + b
        return (s + jnp.where(even, pltpu.roll(s, LANES - 1, 1), pltpu.roll(s, 1, 1))) * 0.25

    return each(one, low, high)


def average_even(low, high):
    def one(a, b):
        s = a + b
        return (s + pltpu.roll(s, LANES - 1, 1)) * 0.25

    return tuple(each(one, a, b) for a, b in zip(low, high))


def average3(low, high):
    return tuple(average(a, b) for a, b in zip(low, high))


def interleave(x, y):
    even = lane_ids() % 2 == 0
    return tuple(each(lambda a, b: jnp.where(even, a, b), p, q) for p, q in zip(x, y))


def difference(z):
    even = lane_ids() % 2 == 0
    one = lambda a: jnp.where(even, a - pltpu.roll(a, LANES - 1, 1), pltpu.roll(a, 1, 1) - a)
    return tuple(each(one, row) for row in z)


def added(x, y):
    return tuple(each(jnp.add, a, b) for a, b in zip(x, y))


def rows_of(ref, *at):
    return [ref[(*at, j)] for j in range(ref.shape[-3])]


def put(ref, at, row):
    for j, a in enumerate(row):
        ref[(*at, j)] = a


def three(ref, at):
    return tuple(rows_of(ref, at, k) for k in range(3))


def put_three(ref, at, rows):
    for k, row in enumerate(rows):
        put(ref, (at, k), row)


def masked(rows, factor):
    e, u, v = rows
    return [a * factor for a in e], u, v


def turning(row, first_row, scale, all_rows, dt):
    y = (first_row + row).astype(jnp.float32) * (2.0 * scale) + scale
    return (dt * CORIOLIS / DIFFUSION) * (y * (1.0 / all_rows) - 1.0)


def in_tiles(nj, row, j):
    tile = nj * SUB * SUB
    return pl.ds((row // SUB) * tile + row % SUB + j * SUB, SUB, stride=nj * SUB)


SCALE = (4.0, 2.0, 2.0)


def emit(ref, at, nj, row, rows):
    for k in range(3):
        for j in range(nj):
            ref[(*at, k, in_tiles(nj, row, j))] = rows[k][j] * (1.0 / SCALE[k])


def wetness(mask):
    return mask.astype(jnp.float32) * DIFFUSION


def pack_kernel(nj, initial, depth, mask, out, initial_v, depth_v, mask_v, sems):
    lane = lax.axis_index("cuts")
    wide = nj * SUB

    def fill(tile, at, row_of):
        there = pl.ds(tile, wide), pl.ds(at, HALO)
        copies = [
            pltpu.make_async_copy(initial.at[:, *there, :], initial_v, sems.at[0]),
            pltpu.make_async_copy(depth.at[*there, :], depth_v, sems.at[1]),
            pltpu.make_async_copy(mask.at[*there, :], mask_v, sems.at[2]),
        ]
        for copy in copies:
            copy.start()
        for copy in copies:
            copy.wait()
        flat = [ref.reshape(*ref.shape[:-3], wide * HALO, LANES) for ref in (initial_v, depth_v, mask_v)]
        for d in range(HALO):
            for j in range(nj):
                at = pl.ds(row_of(d) + j * HALO, SUB, stride=nj * HALO)
                for k in range(3):
                    out[d * PER + k, j] = flat[0][k, at, :] * SCALE[k]
                out[d * PER + 3, j] = flat[1][at, :] * 4.0
                if d < HALO - 1:
                    out[d * PER + 4, j] = wetness(flat[2][at, :])

    pl.when(lane == 0)(lambda: fill(0, 0, lambda d: d))
    pl.when(lane != 0)(lambda: fill(depth.shape[0] - wide, SUB - HALO, lambda d: HALO - 1 - d))


def sideways(h, cols):
    lane = lane_ids()
    return next_col(h, cols, lane >= LANES - cols), prev_col(h, cols, lane < cols)


def middle_kernel(nj, bricks, initial, depth, mask, tiles, ini, hw, s1, rc, rhw, rf, c1, p1, s2, dif):
    lane = lax.axis_index("cuts")
    brick = lax.axis_index("brick")
    n = ini.shape[0]
    m = n // 2
    all_rows = n * bricks
    tile = nj * SUB * SUB
    parts = n // SUB

    def load(t):
        for r in range(SUB):
            row = t * SUB + r
            high = []
            for j in range(nj):
                at = pl.ds(t * tile + r + j * SUB, SUB, stride=nj * SUB)
                for k in range(3):
                    ini[row, k, j] = initial[k, at, :] * SCALE[k]
                high.append(depth[at, :] * 4.0)
                hw[row, 1, j] = wetness(mask[at, :])
            put(hw, (row, 0), high)
            for k, side in enumerate(sideways(high, 1)):
                put(hw, (row, 2 + k), side)

    for t in range(parts):
        load(t)

    def fine(states, row, count):
        return steps(
            states,
            [rows_of(hw, row + d, 0) for d in range(-1, count + 1)],
            [rows_of(hw, row + d, 1) for d in range(count)],
            [turning(row + d, brick * n, 1.0, all_rows, FINE_TIME) for d in range(count)],
            FINE_TIME,
            1,
            [(rows_of(hw, row + d, 2), rows_of(hw, row + d, 3)) for d in range(count)],
        )

    def around(ref, row, count):
        return [three(ref, row + d) for d in range(-1, count + 1)]

    def coarse(states, row, count):
        return steps(
            states,
            [rows_of(rhw, row + d, 0) for d in range(-1, count + 1)],
            [rows_of(rhw, row + d, 1) for d in range(count)],
            [turning(row + d, brick * m, 2.0, all_rows, COARSE_TIME) for d in range(count)],
            COARSE_TIME,
            2,
            [(rows_of(rhw, row + d, 2), rows_of(rhw, row + d, 3)) for d in range(count)],
        )

    def store(ref, row, new):
        for d, rows in enumerate(new):
            put_three(ref, row + d, rows)

    store(s1, 1, fine(around(ini, 1, n - 2), 1, n - 2))
    store(s2, 2, fine(around(s1, 2, n - 4), 2, n - 4))

    @pl.when(lane == 0)
    def _():
        def copied(row, count):
            for d in range(count):
                emit(tiles, (), nj, row + d, three(s2, row + d))

        copied(2, n - 4)

    @pl.when(lane != 0)
    def _():
        def restrict(row, count):
            for d in range(count):
                low, high = 2 * (row + d), 2 * (row + d) + 1
                put_three(rc, row + d, average3(three(ini, low), three(ini, high)))

        def restrict_depth(row, count):
            for d in range(count):
                low, high = 2 * (row + d), 2 * (row + d) + 1
                deep = average(rows_of(hw, low, 0), rows_of(hw, high, 0))
                dry = average(rows_of(hw, low, 1), rows_of(hw, high, 1))
                for k, x in enumerate((deep, dry, *sideways(deep, 2))):
                    put(rhw, (row + d, k), x)

        restrict(0, m)
        restrict_depth(0, m)
        store(c1, 1, coarse(around(rc, 1, m - 2), 1, m - 2))

        def again(row, count):
            for d in range(count):
                low, high = 2 * (row + d), 2 * (row + d) + 1
                put_three(rf, row + d, average_even(three(s2, low), three(s2, high)))

        again(1, m - 2)

        def correct(row, count):
            both = [interleave(a, b) for a, b in zip(around(rf, row, count), around(c1, row, count))]
            store(dif, row, [difference(z) for z in coarse(both, row, count)])

        correct(2, m - 4)

        def prolonged(half, count):
            pairs = around(c1, half, count)
            twice = [pairs[(d + 1) // 2] for d in range(2 * count + 2)]
            store(p1, 2 * half, fine(twice, 2 * half, 2 * count))

        prolonged(2, m - 4)
        for row in (3, n - 4):
            store(p1, row, fine([three(c1, (row + d) // 2) for d in (-1, 0, 1)], row, 1))

        def last(row, count):
            for d, rows in enumerate(fine(around(p1, row, count), row, count)):
                emit(tiles, (), nj, row + d, added(rows, three(dif, (row + d) // 2)))

        last(4, n - 8)


def edge_kernel(nj, bricks, n, turned, near, ini, hw, s1, rc, rhw, rf, c1, p1, *refs):
    lane = lax.axis_index("cuts")
    brick = lax.axis_index("brick")
    all_rows = n * bricks
    m = n // 2
    wide = nj * SUB
    if turned:
        ready, _, out, tiles, sems = refs
    else:
        middle, out, tiles, sems = refs

    def own(s, i, count):
        return i if s == 0 else count - 1 - i

    def depth(s, i):
        return rows_of(near, (-1 - i) * PER + 3) if i < 0 else rows_of(hw, own(s, i, n), 0)

    def wet(s, i):
        return rows_of(near, (-1 - i) * PER + 4) if i < 0 else rows_of(hw, own(s, i, n), 1)

    def initial(s, i):
        if i < 0:
            return tuple(rows_of(near, (-1 - i) * PER + k) for k in range(3))
        return three(ini, own(s, i, n))

    def known(ref, s, ids):
        return {i: three(ref, own(s, i, ref.shape[0])) for i in ids}

    def inside(s):
        there = brick > 0 if s == 0 else brick < bricks - 1
        return jnp.where(there, 1.0, 0.0).astype(jnp.float32)

    def advance(s, ids, state, heights, wets, turn, dt, cols, beside):
        run = list(ids) if s == 0 else list(ids)[::-1]
        way = 1 if s == 0 else -1
        span = [run[0] - way, *run, run[-1] + way]
        sides = [beside(i) for i in run]
        new = steps([state(i) for i in span], [heights(i) for i in span], [wets(i) for i in run], [turn(i) for i in run], dt, cols, sides)
        return {i: masked(x, inside(s)) if i < 0 else x for i, x in zip(run, new)}

    def fine(s, ids, state, beside):
        turn = lambda i: turning(jnp.int32(own(s, i, n)), brick * n, 1.0, all_rows, FINE_TIME)
        return advance(s, ids, state, lambda i: depth(s, i), lambda i: wet(s, i), turn, FINE_TIME, 1, beside)

    def coarse(s, ids, state, deep, dry, beside):
        turn = lambda i: turning(jnp.int32(own(s, i, m)), brick * m, 2.0, all_rows, COARSE_TIME)
        return advance(s, ids, state, deep.__getitem__, dry.__getitem__, turn, COARSE_TIME, 2, beside.__getitem__)

    def sides_from(s, outer):
        held = {i: sideways(depth(s, i), 1) for i in range(outer, 0)}
        return lambda i: held[i] if i < 0 else (rows_of(hw, own(s, i, n), 2), rows_of(hw, own(s, i, n), 3))

    def flown(s, outer, beside):
        start = {i: initial(s, i) for i in range(outer - 2, 2)}
        one = fine(s, range(outer - 1, 1), start.__getitem__, beside)
        one.update(known(s1, s, (1, 2)))
        return fine(s, range(outer, 2), one.__getitem__, beside)

    def sent(ref, s, count, sem):
        at = 0 if s == 0 else SUB - count
        where = 0 if s == 0 else (n // SUB - 1) * wide
        src = ref.reshape(3, wide, SUB, LANES).at[:, :, at : at + count, :]
        return pltpu.make_async_copy(src, out.at[:, where : where + wide, at : at + count, :], sems.at[sem])

    def earlier(s, count):
        return sent(ready, 1 - s, count, 0) if turned else pltpu.make_async_copy(middle, out, sems.at[0])

    def finished(s, count, rows_of_side):
        for i, x in rows_of_side().items():
            if i >= 0:
                emit(tiles, (), nj, own(s, i, SUB), x)
        if turned:
            later = sent(tiles, s, count, 1)
            later.start()
            later.wait()
        earlier(s, count).wait()

    def first_end(s):
        return flown(s, 0, sides_from(s, -1))

    def second_end(s):
        beside = sides_from(s, -3)
        start = {i: average3(initial(s, 2 * i), initial(s, 2 * i + 1)) for i in (-2, -1)}
        start.update(known(rc, s, (0, 1)))
        deep = {i: average(depth(s, 2 * i), depth(s, 2 * i + 1)) for i in (-2, -1)}
        deep.update({i: rows_of(rhw, own(s, i, m), 0) for i in (0, 1, 2)})
        dry = {-1: average(wet(s, -2), wet(s, -1))}
        dry.update({i: rows_of(rhw, own(s, i, m), 1) for i in (0, 1)})
        aside = {-1: sideways(deep[-1], 2)}
        aside.update({i: (rows_of(rhw, own(s, i, m), 2), rows_of(rhw, own(s, i, m), 3)) for i in (0, 1)})
        first = coarse(s, (-1, 0), start.__getitem__, deep, dry, aside)
        first.update(known(c1, s, (1, 2)))
        one = fine(s, range(-1, 3), lambda i: first[i // 2], beside)
        one.update(known(p1, s, (3, 4)))
        last = fine(s, range(4), one.__getitem__, beside)
        two = flown(s, -2, beside)
        fresh = {i: average_even(two[2 * i], two[2 * i + 1]) for i in (-1, 0)}
        fresh.update(known(rf, s, (1, 2)))
        both = {i: interleave(fresh[i], first[i]) for i in range(-1, 3)}
        add = {i: difference(z) for i, z in coarse(s, (0, 1), both.__getitem__, deep, dry, aside).items()}
        return {i: added(x, add[i // 2]) for i, x in last.items()}

    one, two = int(turned), 1 - int(turned)
    pl.when(lane == 0)(lambda: earlier(one, 2).start())
    pl.when(lane != 0)(lambda: earlier(two, 4).start())
    pl.when(lane == 0)(lambda: finished(one, 2, lambda: first_end(one)))
    pl.when(lane != 0)(lambda: finished(two, 4, lambda: second_end(two)))


def tiled(a):
    *lead, rows, cols = a.shape
    a = a.reshape(*lead, rows // SUB, SUB, cols // LANES, LANES)
    return jnp.swapaxes(a, -3, -2).reshape(*lead, rows * cols // LANES, LANES)


def untiled(a, rows, cols):
    lead = a.shape[:-2]
    a = a.reshape(*lead, rows // SUB, cols // LANES, SUB, LANES)
    return jnp.swapaxes(a, -3, -2).reshape(*lead, rows, cols)


def shards(initial, depth, mask):
    bricks = lax.axis_size("brick")
    n, cols = depth.shape
    nj = cols // (SUB * LANES)
    row = (nj, SUB, LANES)
    f32 = jnp.float32
    initial, depth, mask = tiled(initial), tiled(depth), tiled(mask)
    tile = nj * SUB * SUB
    size = depth.shape[0]
    params = pltpu.CompilerParams(vmem_limit_bytes=VMEM_LIMIT)
    far = pl.BlockSpec(memory_space=pltpu.HBM)
    local = pl.BlockSpec(memory_space=pltpu.VMEM)

    def hold(rows, count):
        return jax.ShapeDtypeStruct((rows, count, *row), f32)

    def rows8(a):
        return a.reshape(*a.shape[:-2], -1, SUB, LANES)

    wide = nj * SUB
    packed = pl.pallas_call(
        functools.partial(pack_kernel, nj),
        out_shape=jax.ShapeDtypeStruct((PACKED, *row), f32),
        in_specs=[far] * 3,
        out_specs=local,
        scratch_shapes=[
            pltpu.VMEM((3, wide, HALO, LANES), f32),
            pltpu.VMEM((wide, HALO, LANES), f32),
            pltpu.VMEM((wide, HALO, LANES), jnp.int32),
            pltpu.SemaphoreType.DMA((3,)),
        ],
        compiler_params=params,
        name="pack",
    )(*(pltpu.with_memory_space_constraint(rows8(a), pltpu.HBM) for a in (initial, depth, mask)))
    packed, initial, depth, mask = lax.optimization_barrier((packed, initial, depth, mask))

    up = [(2 * i + 1, 2 * i + 2) for i in range(bricks - 1)]
    near = lax.ppermute(packed, ("brick", "cuts"), up + [(b, a) for a, b in up])

    inner, *held = pl.pallas_call(
        functools.partial(middle_kernel, nj, bricks),
        out_shape=[
            jax.ShapeDtypeStruct((3, size, LANES), f32),
            hold(n, 3),
            hold(n, 4),
            hold(n, 3),
            hold(n // 2, 3),
            hold(n // 2, 4),
            hold(n // 2, 3),
            hold(n // 2, 3),
            hold(n, 3),
        ],
        in_specs=[local] * 3,
        out_specs=[local] * 9,
        scratch_shapes=[
            pltpu.VMEM((n, 3, *row), f32),
            pltpu.VMEM((n // 2, 3, *row), f32),
        ],
        compiler_params=params,
        cost_estimate=pl.CostEstimate(flops=60 * 5 * n * cols, bytes_accessed=10 * n * cols * 4, transcendentals=0),
        name="middle",
    )(initial, depth, mask)

    def edges(turned, near, *more):
        result = jax.ShapeDtypeStruct((3, size // SUB, SUB, LANES), f32)
        part = jax.ShapeDtypeStruct((3, tile, LANES), f32)
        return pl.pallas_call(
            functools.partial(edge_kernel, nj, bricks, n, turned),
            out_shape=result if turned else [result, part],
            in_specs=[local] * 10 + ([far] if turned else []),
            out_specs=far if turned else [far, local],
            scratch_shapes=[pltpu.VMEM(part.shape, f32)] * turned + [pltpu.SemaphoreType.DMA((2,))],
            input_output_aliases={10: 0} if turned else {},
            compiler_params=params,
            cost_estimate=pl.CostEstimate(flops=60 * n * cols, bytes_accessed=n * cols * 4, transcendentals=0),
            name="edges",
        )(near, *held, *more)

    near, inner, *held = lax.optimization_barrier((near, inner, *held))
    other = lax.ppermute(near, "cuts", [(0, 1), (1, 0)])
    whole, ready = edges(False, near, rows8(inner))
    whole = edges(True, other, ready, whole)
    return untiled(whole.reshape(3, size, LANES), n, cols)[None]


def solution(mesh):
    placed = (P(None, ("grp", "brick"), None), P("brick", None), P("brick", None))
    return jax.shard_map(
        shards,
        mesh=mesh,
        in_specs=placed,
        out_specs=P("cuts", None, ("grp", "brick"), None),
        check_vma=False,
    )
```

```python
import functools

import jax
import jax.numpy as jnp
from jax import lax
from jax.experimental import pallas as pl
from jax.experimental.pallas import tpu as pltpu
from jax.sharding import PartitionSpec as P


COURANT = 0.2
DIFFUSION = 0.05
FRICTION = 0.01
CORIOLIS = 0.5
FINE_TIME = 0.2
COARSE_TIME = 0.4
SUB, LANES = 8, 128
HALO = 4
PER = 5
PACKED = HALO * PER - 1
VMEM_LIMIT = 24 * 1024 * 1024


def next_col(x, amount, edge):
    turned = [pltpu.roll(a, LANES - amount, 1) for a in x]
    turned.append(pltpu.roll(turned[0], SUB - 1, 0))
    return [jnp.where(edge, turned[j + 1], turned[j]) for j in range(len(x))]


def prev_col(x, amount, edge):
    turned = [pltpu.roll(a, amount, 1) for a in x]
    turned.insert(0, pltpu.roll(turned[-1], 1, 0))
    return [jnp.where(edge, turned[j], turned[j + 1]) for j in range(len(x))]


def lane_ids():
    return lax.broadcasted_iota(jnp.int32, (SUB, LANES), 1)


def each(f, *rows):
    return [f(*a) for a in zip(*rows)]


def steps(states, heights, wets, turns, dt, cols, beside):
    lane = lane_ids()
    last, first = lane >= LANES - cols, lane < cols
    k = (1.0 - dt * FRICTION - 4.0 * DIFFUSION) / DIFFUSION
    full = [each(jnp.add, h, s[0]) for h, s in zip(heights, states)]
    flux = [each(jnp.multiply, f, s[1]) for f, s in zip(full, states)]
    out = []
    shifted = None
    for i, (wet, t) in enumerate(zip(wets, turns)):
        (eb, ub, vb), (e, u, v), (ea, ua, va) = states[i : i + 3]
        if shifted is None or states[i + 1] is not states[i]:
            shifted = [(next_col(a, cols, last), prev_col(a, cols, first)) for a in (e, u, v)]
        (e_r, e_l), (u_r, u_l), (v_r, v_l) = shifted
        g_r, g_l = (each(lambda h, a, b: (h + a) * b, *x) for x in zip(beside[i], (e_r, e_l), (v_r, v_l)))
        new_e, new_u, new_v = [], [], []
        for j in range(len(e)):
            spread = ((ea[j] - flux[i + 2][j]) + (eb[j] + flux[i][j])) + ((e_r[j] - g_r[j]) + (e_l[j] + g_l[j]))
            new_e.append(DIFFUSION * (e[j] * (1.0 / DIFFUSION - 4.0) + spread))
            nu = u[j] * (k - (ua[j] - ub[j])) + v[j] * (t - (u_r[j] - u_l[j]))
            nu = nu + (((ua[j] - ea[j]) + (ub[j] + eb[j])) + (u_r[j] + u_l[j]))
            nv = v[j] * (k - (v_r[j] - v_l[j])) - u[j] * (t + (va[j] - vb[j]))
            nv = nv + (((v_r[j] - e_r[j]) + (v_l[j] + e_l[j])) + (va[j] + vb[j]))
            new_u.append(nu * wet[j])
            new_v.append(nv * wet[j])
        out.append((new_e, new_u, new_v))
    return out


def average(low, high):
    even = lane_ids() % 2 == 0

    def one(a, b):
        s = a + b
        return (s + jnp.where(even, pltpu.roll(s, LANES - 1, 1), pltpu.roll(s, 1, 1))) * 0.25

    return each(one, low, high)


def average_even(low, high):
    def one(a, b):
        s = a + b
        return (s + pltpu.roll(s, LANES - 1, 1)) * 0.25

    return tuple(each(one, a, b) for a, b in zip(low, high))


def average3(low, high):
    return tuple(average(a, b) for a, b in zip(low, high))


def interleave(x, y):
    even = lane_ids() % 2 == 0
    return tuple(each(lambda a, b: jnp.where(even, a, b), p, q) for p, q in zip(x, y))


def difference(z):
    even = lane_ids() % 2 == 0
    one = lambda a: jnp.where(even, a - pltpu.roll(a, LANES - 1, 1), pltpu.roll(a, 1, 1) - a)
    return tuple(each(one, row) for row in z)


def added(x, y):
    return tuple(each(jnp.add, a, b) for a, b in zip(x, y))


def rows_of(ref, *at):
    return [ref[(*at, j)] for j in range(ref.shape[-3])]


def put(ref, at, row):
    for j, a in enumerate(row):
        ref[(*at, j)] = a


def three(ref, at):
    return tuple(rows_of(ref, at, k) for k in range(3))


def put_three(ref, at, rows):
    for k, row in enumerate(rows):
        put(ref, (at, k), row)


def masked(rows, factor):
    e, u, v = rows
    return [a * factor for a in e], u, v


def turning(row, first_row, scale, all_rows, dt):
    y = (first_row + row).astype(jnp.float32) * (2.0 * scale) + scale
    return (dt * CORIOLIS / DIFFUSION) * (y * (1.0 / all_rows) - 1.0)


def in_tiles(nj, row, j):
    tile = nj * SUB * SUB
    return pl.ds((row // SUB) * tile + row % SUB + j * SUB, SUB, stride=nj * SUB)


SCALE = (4.0, 2.0, 2.0)


def emit(ref, at, nj, row, rows):
    for k in range(3):
        for j in range(nj):
            ref[(*at, k, in_tiles(nj, row, j))] = rows[k][j] * (1.0 / SCALE[k])


def wetness(mask):
    return mask.astype(jnp.float32) * DIFFUSION


def pack_kernel(nj, initial, depth, mask, out, initial_v, depth_v, mask_v, sems):
    lane = lax.axis_index("cuts")
    wide = nj * SUB

    def fill(tile, at, row_of):
        there = pl.ds(tile, wide), pl.ds(at, HALO)
        parts = [(depth, depth_v), (mask, mask_v)] + [(initial.at[k], initial_v.at[k]) for k in range(3)]
        copies = [pltpu.make_async_copy(src.at[*there, :], dst, sems.at[i]) for i, (src, dst) in enumerate(parts)]
        for copy in copies:
            copy.start()
        forms = [lambda a: a * 4.0, wetness] + [lambda a, k=k: a * SCALE[k] for k in range(3)]
        for place, copy, (_, ref), form in zip((3, 4, 0, 1, 2), copies, parts, forms):
            copy.wait()
            flat = ref.reshape(wide * HALO, LANES)
            for d in range(HALO - 1 if place == 4 else HALO):
                for j in range(nj):
                    out[d * PER + place, j] = form(flat[pl.ds(row_of(d) + j * HALO, SUB, stride=nj * HALO), :])

    pl.when(lane == 0)(lambda: fill(0, 0, lambda d: d))
    pl.when(lane != 0)(lambda: fill(depth.shape[0] - wide, SUB - HALO, lambda d: HALO - 1 - d))


def sideways(h, cols):
    lane = lane_ids()
    return next_col(h, cols, lane >= LANES - cols), prev_col(h, cols, lane < cols)


def middle_kernel(nj, bricks, initial, depth, mask, tiles, ini, hw, s1, rc, rhw, rf, c1, p1, s2, dif):
    lane = lax.axis_index("cuts")
    brick = lax.axis_index("brick")
    n = ini.shape[0]
    m = n // 2
    all_rows = n * bricks
    tile = nj * SUB * SUB
    parts = n // SUB

    def load(t):
        for r in range(SUB):
            row = t * SUB + r
            high = []
            for j in range(nj):
                at = pl.ds(t * tile + r + j * SUB, SUB, stride=nj * SUB)
                for k in range(3):
                    ini[row, k, j] = initial[k, at, :] * SCALE[k]
                high.append(depth[at, :] * 4.0)
                hw[row, 1, j] = wetness(mask[at, :])
            put(hw, (row, 0), high)
            for k, side in enumerate(sideways(high, 1)):
                put(hw, (row, 2 + k), side)

    for t in range(parts):
        load(t)

    def fine(states, row, count):
        return steps(
            states,
            [rows_of(hw, row + d, 0) for d in range(-1, count + 1)],
            [rows_of(hw, row + d, 1) for d in range(count)],
            [turning(row + d, brick * n, 1.0, all_rows, FINE_TIME) for d in range(count)],
            FINE_TIME,
            1,
            [(rows_of(hw, row + d, 2), rows_of(hw, row + d, 3)) for d in range(count)],
        )

    def around(ref, row, count):
        return [three(ref, row + d) for d in range(-1, count + 1)]

    def coarse(states, row, count):
        return steps(
            states,
            [rows_of(rhw, row + d, 0) for d in range(-1, count + 1)],
            [rows_of(rhw, row + d, 1) for d in range(count)],
            [turning(row + d, brick * m, 2.0, all_rows, COARSE_TIME) for d in range(count)],
            COARSE_TIME,
            2,
            [(rows_of(rhw, row + d, 2), rows_of(rhw, row + d, 3)) for d in range(count)],
        )

    def store(ref, row, new):
        for d, rows in enumerate(new):
            put_three(ref, row + d, rows)

    store(s1, 1, fine(around(ini, 1, n - 2), 1, n - 2))
    store(s2, 2, fine(around(s1, 2, n - 4), 2, n - 4))

    @pl.when(lane == 0)
    def _():
        def copied(row, count):
            for d in range(count):
                emit(tiles, (), nj, row + d, three(s2, row + d))

        copied(2, n - 4)

    @pl.when(lane != 0)
    def _():
        def restrict(row, count):
            for d in range(count):
                low, high = 2 * (row + d), 2 * (row + d) + 1
                put_three(rc, row + d, average3(three(ini, low), three(ini, high)))

        def restrict_depth(row, count):
            for d in range(count):
                low, high = 2 * (row + d), 2 * (row + d) + 1
                deep = average(rows_of(hw, low, 0), rows_of(hw, high, 0))
                dry = average(rows_of(hw, low, 1), rows_of(hw, high, 1))
                for k, x in enumerate((deep, dry, *sideways(deep, 2))):
                    put(rhw, (row + d, k), x)

        restrict(0, m)
        restrict_depth(0, m)
        store(c1, 1, coarse(around(rc, 1, m - 2), 1, m - 2))

        def again(row, count):
            for d in range(count):
                low, high = 2 * (row + d), 2 * (row + d) + 1
                put_three(rf, row + d, average_even(three(s2, low), three(s2, high)))

        again(1, m - 2)

        def correct(row, count):
            both = [interleave(a, b) for a, b in zip(around(rf, row, count), around(c1, row, count))]
            store(dif, row, [difference(z) for z in coarse(both, row, count)])

        correct(2, m - 4)

        def prolonged(half, count):
            pairs = around(c1, half, count)
            twice = [pairs[(d + 1) // 2] for d in range(2 * count + 2)]
            store(p1, 2 * half, fine(twice, 2 * half, 2 * count))

        prolonged(2, m - 4)
        for row in (3, n - 4):
            store(p1, row, fine([three(c1, (row + d) // 2) for d in (-1, 0, 1)], row, 1))

        def last(row, count):
            for d, rows in enumerate(fine(around(p1, row, count), row, count)):
                emit(tiles, (), nj, row + d, added(rows, three(dif, (row + d) // 2)))

        last(4, n - 8)


def edge_kernel(nj, bricks, n, turned, near, ini, hw, s1, rc, rhw, rf, c1, p1, *refs):
    lane = lax.axis_index("cuts")
    brick = lax.axis_index("brick")
    all_rows = n * bricks
    m = n // 2
    wide = nj * SUB
    if turned:
        ready, _, out, tiles, sems = refs
    else:
        middle, out, tiles, sems = refs

    def own(s, i, count):
        return i if s == 0 else count - 1 - i

    def depth(s, i):
        return rows_of(near, (-1 - i) * PER + 3) if i < 0 else rows_of(hw, own(s, i, n), 0)

    def wet(s, i):
        return rows_of(near, (-1 - i) * PER + 4) if i < 0 else rows_of(hw, own(s, i, n), 1)

    def initial(s, i):
        if i < 0:
            return tuple(rows_of(near, (-1 - i) * PER + k) for k in range(3))
        return three(ini, own(s, i, n))

    def known(ref, s, ids):
        return {i: three(ref, own(s, i, ref.shape[0])) for i in ids}

    def inside(s):
        there = brick > 0 if s == 0 else brick < bricks - 1
        return jnp.where(there, 1.0, 0.0).astype(jnp.float32)

    def advance(s, ids, state, heights, wets, turn, dt, cols, beside):
        run = list(ids) if s == 0 else list(ids)[::-1]
        way = 1 if s == 0 else -1
        span = [run[0] - way, *run, run[-1] + way]
        sides = [beside(i) for i in run]
        new = steps([state(i) for i in span], [heights(i) for i in span], [wets(i) for i in run], [turn(i) for i in run], dt, cols, sides)
        return {i: masked(x, inside(s)) if i < 0 else x for i, x in zip(run, new)}

    def fine(s, ids, state, beside):
        turn = lambda i: turning(jnp.int32(own(s, i, n)), brick * n, 1.0, all_rows, FINE_TIME)
        return advance(s, ids, state, lambda i: depth(s, i), lambda i: wet(s, i), turn, FINE_TIME, 1, beside)

    def coarse(s, ids, state, deep, dry, beside):
        turn = lambda i: turning(jnp.int32(own(s, i, m)), brick * m, 2.0, all_rows, COARSE_TIME)
        return advance(s, ids, state, deep.__getitem__, dry.__getitem__, turn, COARSE_TIME, 2, beside.__getitem__)

    def sides_from(s, outer):
        held = {i: sideways(depth(s, i), 1) for i in range(outer, 0)}
        return lambda i: held[i] if i < 0 else (rows_of(hw, own(s, i, n), 2), rows_of(hw, own(s, i, n), 3))

    def flown(s, outer, beside):
        start = {i: initial(s, i) for i in range(outer - 2, 2)}
        one = fine(s, range(outer - 1, 1), start.__getitem__, beside)
        one.update(known(s1, s, (1, 2)))
        return fine(s, range(outer, 2), one.__getitem__, beside)

    def sent(ref, s, count, sem):
        at = 0 if s == 0 else SUB - count
        where = 0 if s == 0 else (n // SUB - 1) * wide
        src = ref.reshape(3, wide, SUB, LANES).at[:, :, at : at + count, :]
        return pltpu.make_async_copy(src, out.at[:, where : where + wide, at : at + count, :], sems.at[sem])

    def earlier(s, count):
        return sent(ready, 1 - s, count, 0) if turned else pltpu.make_async_copy(middle, out, sems.at[0])

    def finished(s, count, rows_of_side):
        for i, x in rows_of_side().items():
            if i >= 0:
                emit(tiles, (), nj, own(s, i, SUB), x)
        if turned:
            later = sent(tiles, s, count, 1)
            later.start()
            later.wait()
        earlier(s, count).wait()

    def first_end(s):
        return flown(s, 0, sides_from(s, -1))

    def second_end(s):
        beside = sides_from(s, -3)
        start = {i: average3(initial(s, 2 * i), initial(s, 2 * i + 1)) for i in (-2, -1)}
        start.update(known(rc, s, (0, 1)))
        deep = {i: average(depth(s, 2 * i), depth(s, 2 * i + 1)) for i in (-2, -1)}
        deep.update({i: rows_of(rhw, own(s, i, m), 0) for i in (0, 1, 2)})
        dry = {-1: average(wet(s, -2), wet(s, -1))}
        dry.update({i: rows_of(rhw, own(s, i, m), 1) for i in (0, 1)})
        aside = {-1: sideways(deep[-1], 2)}
        aside.update({i: (rows_of(rhw, own(s, i, m), 2), rows_of(rhw, own(s, i, m), 3)) for i in (0, 1)})
        first = coarse(s, (-1, 0), start.__getitem__, deep, dry, aside)
        first.update(known(c1, s, (1, 2)))
        one = fine(s, range(-1, 3), lambda i: first[i // 2], beside)
        one.update(known(p1, s, (3, 4)))
        last = fine(s, range(4), one.__getitem__, beside)
        two = flown(s, -2, beside)
        fresh = {i: average_even(two[2 * i], two[2 * i + 1]) for i in (-1, 0)}
        fresh.update(known(rf, s, (1, 2)))
        both = {i: interleave(fresh[i], first[i]) for i in range(-1, 3)}
        add = {i: difference(z) for i, z in coarse(s, (0, 1), both.__getitem__, deep, dry, aside).items()}
        return {i: added(x, add[i // 2]) for i, x in last.items()}

    one, two = int(turned), 1 - int(turned)
    pl.when(lane == 0)(lambda: earlier(one, 2).start())
    pl.when(lane != 0)(lambda: earlier(two, 4).start())
    pl.when(lane == 0)(lambda: finished(one, 2, lambda: first_end(one)))
    pl.when(lane != 0)(lambda: finished(two, 4, lambda: second_end(two)))


def tiled(a):
    *lead, rows, cols = a.shape
    a = a.reshape(*lead, rows // SUB, SUB, cols // LANES, LANES)
    return jnp.swapaxes(a, -3, -2).reshape(*lead, rows * cols // LANES, LANES)


def untiled(a, rows, cols):
    lead = a.shape[:-2]
    a = a.reshape(*lead, rows // SUB, cols // LANES, SUB, LANES)
    return jnp.swapaxes(a, -3, -2).reshape(*lead, rows, cols)


def shards(initial, depth, mask):
    bricks = lax.axis_size("brick")
    n, cols = depth.shape
    nj = cols // (SUB * LANES)
    row = (nj, SUB, LANES)
    f32 = jnp.float32
    initial, depth, mask = tiled(initial), tiled(depth), tiled(mask)
    tile = nj * SUB * SUB
    size = depth.shape[0]
    params = pltpu.CompilerParams(vmem_limit_bytes=VMEM_LIMIT)
    far = pl.BlockSpec(memory_space=pltpu.HBM)
    local = pl.BlockSpec(memory_space=pltpu.VMEM)

    def hold(rows, count):
        return jax.ShapeDtypeStruct((rows, count, *row), f32)

    def rows8(a):
        return a.reshape(*a.shape[:-2], -1, SUB, LANES)

    wide = nj * SUB
    packed = pl.pallas_call(
        functools.partial(pack_kernel, nj),
        out_shape=jax.ShapeDtypeStruct((PACKED, *row), f32),
        in_specs=[far] * 3,
        out_specs=local,
        scratch_shapes=[
            pltpu.VMEM((3, wide, HALO, LANES), f32),
            pltpu.VMEM((wide, HALO, LANES), f32),
            pltpu.VMEM((wide, HALO, LANES), jnp.int32),
            pltpu.SemaphoreType.DMA((5,)),
        ],
        compiler_params=params,
        name="pack",
    )(*(pltpu.with_memory_space_constraint(rows8(a), pltpu.HBM) for a in (initial, depth, mask)))
    packed, initial, depth, mask = lax.optimization_barrier((packed, initial, depth, mask))

    up = [(2 * i + 1, 2 * i + 2) for i in range(bricks - 1)]
    near = lax.ppermute(packed, ("brick", "cuts"), up + [(b, a) for a, b in up])

    inner, *held = pl.pallas_call(
        functools.partial(middle_kernel, nj, bricks),
        out_shape=[
            jax.ShapeDtypeStruct((3, size, LANES), f32),
            hold(n, 3),
            hold(n, 4),
            hold(n, 3),
            hold(n // 2, 3),
            hold(n // 2, 4),
            hold(n // 2, 3),
            hold(n // 2, 3),
            hold(n, 3),
        ],
        in_specs=[local] * 3,
        out_specs=[local] * 9,
        scratch_shapes=[
            pltpu.VMEM((n, 3, *row), f32),
            pltpu.VMEM((n // 2, 3, *row), f32),
        ],
        compiler_params=params,
        cost_estimate=pl.CostEstimate(flops=60 * 5 * n * cols, bytes_accessed=10 * n * cols * 4, transcendentals=0),
        name="middle",
    )(initial, depth, mask)

    def edges(turned, near, *more):
        result = jax.ShapeDtypeStruct((3, size // SUB, SUB, LANES), f32)
        part = jax.ShapeDtypeStruct((3, tile, LANES), f32)
        return pl.pallas_call(
            functools.partial(edge_kernel, nj, bricks, n, turned),
            out_shape=result if turned else [result, part],
            in_specs=[local] * 10 + ([far] if turned else []),
            out_specs=far if turned else [far, local],
            scratch_shapes=[pltpu.VMEM(part.shape, f32)] * turned + [pltpu.SemaphoreType.DMA((2,))],
            input_output_aliases={10: 0} if turned else {},
            compiler_params=params,
            cost_estimate=pl.CostEstimate(flops=60 * n * cols, bytes_accessed=n * cols * 4, transcendentals=0),
            name="edges",
        )(near, *held, *more)

    near, inner, *held = lax.optimization_barrier((near, inner, *held))
    other = lax.ppermute(near, "cuts", [(0, 1), (1, 0)])
    whole, ready = edges(False, near, rows8(inner))
    whole = edges(True, other, ready, whole)
    return untiled(whole.reshape(3, size, LANES), n, cols)[None]


def solution(mesh):
    placed = (P(None, ("grp", "brick"), None), P("brick", None), P("brick", None))
    return jax.shard_map(
        shards,
        mesh=mesh,
        in_specs=placed,
        out_specs=P("cuts", None, ("grp", "brick"), None),
        check_vma=False,
    )
```
